32 devices in a mesh: row: 8 (over z, x), col: 4 (over y, core).
Axes of the slice: x: 2, y: 2, z: 4, core: 2. Of those that a mesh axis runs over, the one named last changes fastest.
Arguments:
- tiles: bfloat16 [8, 96, 256, 256], P('row', 'col'), may hold values from -0.109375 to 0.109375
- tile_slot: int32 [8, 96], P('row', 'col'), may hold values from 0 to 31
- tile_count: int32 [8, 4], P('row', 'col'), may hold values from 1 to 24, 48 in all within a row
- feats: bfloat16 [8192, 256], P('col'), may hold values from -6 to 6
- weight: bfloat16 [256, 256], replicated, may hold values from -0.375 to 0.375
- out_grad: bfloat16 [8192, 256], P(('row', 'col')), may hold values from -6 to 6
Outputs:
- activated: bfloat16 [8192, 256], P(('row', 'col'))
- weight_grad: float32 [256, 256], replicated
- window_grad: bfloat16 [4, 2048, 256], P('col', 'row')
The draws below stay inside these ranges and needn't reach their ends.
Inputs may be any that keep to these rules, and one draw needn't show every extreme that they name: `tile_count`: some block in every draw has all 24 slots in use.
All inputs are finite; a program needn't handle non-finite values.
Results may differ from the reference program's by a relative error of at most 0.0065.
Values may be sent and summed in bfloat16 or wider, within the bound.
A program may use at most 64 MiB of HBM per device.

```python
import math
import jax
import jax.numpy as jnp
import numpy as np
from jax import lax

F = 256
TILE = 256
TPD = 24
RT = 4
CT = 8
NODES = 8192
WCOLS = 8192
N_ROW = 8
N_COL = 4


def set_ends(result, rng, low, top_value):
    spot = [jax.random.randint(jax.random.fold_in(rng, axis), (), 0, length) for axis, length in enumerate(result.shape)]
    longest = result.shape.index(max(result.shape))
    next_to = spot[:longest] + [(spot[longest] + 1) % result.shape[longest]] + spot[longest + 1:]
    return result.at[tuple(spot)].set(low).at[tuple(next_to)].set(top_value)


def steps_of(stream_key, dims, shards, low, largest):
    gain, own = 1.0, jax.random.fold_in(stream_key, 6)
    for axis_at, parts in shards:
        steps = jnp.exp(jax.random.uniform(jax.random.fold_in(own, axis_at), (parts,), jnp.float32, low / len(shards), largest / len(shards)))
        gain = gain * jnp.repeat(steps, dims[axis_at] // parts).reshape([-1 if axis == axis_at else 1 for axis in range(len(dims))])
    return gain


def length_profile(count, total, limit, lean):
    loads = [(1 << 20) // math.isqrt(grade ** lean) + 1 for grade in range(2, count + 1)]
    surplus, given = total - limit - (count - 1), [1] * (count - 1)
    while surplus > 0:
        movable = [i for i in range(count - 1) if given[i] < limit]
        pool, budget = sum([loads[i] for i in movable]), surplus
        for i in movable:
            more = min(limit - given[i], max(1, budget * loads[i] // pool), surplus)
            given[i] = given[i] + more
            surplus = surplus - more
    return np.array([limit] + given)


def ragged(own_key, number_of, total, most, lean):
    if number_of == 2:
        one = jax.random.randint(own_key, (), max(1, total - most), min(most, total - 1) + 1)
        return jnp.stack([one, total - one])
    tallies = jnp.asarray(length_profile(number_of, total, most, lean), jnp.int32)
    couples = (number_of - 1) // 2
    source_of, sink = tallies[1:1 + 2 * couples:2], tallies[2:2 + 2 * couples:2]
    margin = jnp.minimum(source_of - 1, most - sink)
    moved = jax.random.randint(jax.random.fold_in(own_key, 1), (couples,), 0, 1 << 20) % (margin + 1)
    tallies = tallies.at[1:1 + 2 * couples:2].set(source_of - moved).at[2:2 + 2 * couples:2].set(sink + moved)
    return tallies[jax.random.permutation(jax.random.fold_in(own_key, 2), number_of)]


def centred(stream_key, shape, width, most, split=(), kind=jnp.bfloat16):
    result = width * jax.random.normal(stream_key, shape, jnp.float32)
    if split:
        result = result * steps_of(stream_key, shape, split, -0.22, 0.18)
    return jnp.clip(result, -most, most).astype(kind)


def setup_inputs(seed: int = 0) -> dict:
    seeds = jax.random.split(jax.random.key(seed), 7)
    return {
        "tiles": centred(seeds[0], (N_ROW, N_COL * TPD, TILE, TILE), (TILE * N_COL * TPD // (2 * RT)) ** -0.5, 0.109375, ((0, 8), (1, 4))),
        "tile_slot": set_ends(jax.random.randint(seeds[1], (N_ROW, N_COL * TPD), 0, RT * CT), jax.random.fold_in(seeds[1], 1), 0, (RT * CT) - 1).astype(jnp.int32),
        "tile_count": jax.vmap(lambda own: ragged(own, N_COL, N_COL * TPD // 2, TPD, 2))(jax.random.split(seeds[2], N_ROW)).reshape((N_ROW, N_COL)).astype(jnp.int32),
        "feats": centred(seeds[3], (WCOLS, F), 1.0, 6.0, ((0, 4),)),
        "weight": centred(seeds[4], (F, F), F ** -0.5, 0.375),
        "out_grad": centred(seeds[5], (NODES, F), 1.0, 6.0, ((0, 32),)),
    }


def reference(tiles, tile_slot, tile_count, feats, weight, out_grad):
    highest = lax.Precision.HIGHEST
    block_tiles = tiles.reshape(N_ROW, N_COL, TPD, TILE, TILE)
    slot_rows = tile_slot.reshape(N_ROW, N_COL, TPD)
    feature_tiles = feats.reshape(N_COL, CT, TILE, F)
    column_ids = jnp.arange(N_COL)[:, None]

    def forward_row(running, inputs):
        blocks, slots, counts = inputs
        col_index = slots % CT
        row_index = slots // CT
        chosen = feature_tiles[column_ids, col_index]
        products = jnp.einsum("ctij,ctjf->ctif", blocks.astype(jnp.float32), chosen.astype(jnp.float32), precision=highest)
        live_mask = (jnp.arange(TPD)[None, :] < counts[:, None]).astype(jnp.float32)
        onehot = (row_index[..., None] == jnp.arange(RT)).astype(jnp.float32) * live_mask[..., None]
        return running, jnp.einsum("ctk,ctif->kif", onehot, products, precision=highest)

    unused, sums = lax.scan(forward_row, jnp.float32(0.0), (block_tiles, slot_rows, tile_count))
    aggregated = sums.reshape(NODES, F).astype(jnp.bfloat16)
    pre_act = jnp.dot(aggregated, weight, preferred_element_type=jnp.float32)
    sigmoid_pre = jax.nn.sigmoid(pre_act)
    activated = (pre_act * sigmoid_pre).astype(jnp.bfloat16)
    grad_pre = (out_grad.astype(jnp.float32) * sigmoid_pre * (1.0 + pre_act * (1.0 - sigmoid_pre))).astype(jnp.bfloat16)
    weight_grad = lax.dot_general(aggregated, grad_pre, (((0,), (0,)), ((), ())), preferred_element_type=jnp.float32) * (float(NODES) ** -0.5)
    grad_agg = jnp.dot(grad_pre, weight.T, preferred_element_type=jnp.float32).astype(jnp.bfloat16)
    grad_tiles = grad_agg.reshape(N_ROW, RT, TILE, F)

    def backward_row(running, inputs):
        blocks, slots, counts, grads = inputs
        col_index = slots % CT
        row_index = slots // CT
        chosen = grads[row_index]
        products = jnp.einsum("ctij,ctif->ctjf", blocks.astype(jnp.float32), chosen.astype(jnp.float32), precision=highest)
        live_mask = (jnp.arange(TPD)[None, :] < counts[:, None]).astype(jnp.float32)
        onehot = (col_index[..., None] == jnp.arange(CT)).astype(jnp.float32) * live_mask[..., None]
        return running + jnp.einsum("ctk,ctjf->ckjf", onehot, products, precision=highest), jnp.float32(0.0)

    start = jnp.zeros((N_COL, CT, TILE, F), jnp.float32)
    window_sum, unused_two = lax.scan(backward_row, start, (block_tiles, slot_rows, tile_count, grad_tiles))
    window_grad = window_sum.reshape(N_COL, CT * TILE, F).astype(jnp.bfloat16)
    return activated, weight_grad, window_grad
```

```python
import functools
import math

import jax
import jax.numpy as jnp
from jax import lax
from jax.experimental import pallas as pl
from jax.experimental.pallas import tpu as pltpu
from jax.sharding import PartitionSpec as P

RT = 4
LANES = 128
MESH = pl.DeviceIdType.MESH
F32 = jnp.float32
BF16 = jnp.bfloat16


def block_kernel(slots, count, tiles, feats, block, partial, dense, extra, source, total,
                 first, others, following, tile_sem, feat_sem, out_sem):
    size = tiles.shape[1]
    col_tiles = feats.shape[0] // size
    places = RT * col_tiles
    live = count[0]

    feat_copy = pltpu.make_async_copy(feats, source, feat_sem)
    feat_copy.start()

    def place_of(slot):
        row = pl.multiple_of(slot // col_tiles * size, size)
        column = pl.multiple_of(slot % col_tiles * size, size)
        return dense.at[pl.ds(row, size), pl.ds(column, size)]

    @pl.loop(0, places)
    def _(place):
        first[place] = -1
        others[place] = -1

    @pl.loop(0, live)
    def _(position):
        slot = slots[position]
        taken = first[slot] >= 0

        @pl.when(jnp.logical_not(taken))
        def _():
            first[slot] = position
            pltpu.make_async_copy(tiles.at[position], place_of(slot), tile_sem.at[position]).start()

        @pl.when(taken)
        def _():
            following[position] = others[slot]
            others[slot] = position
            pltpu.make_async_copy(
                tiles.at[position], extra.at[position], tile_sem.at[position]
            ).start()

    @pl.loop(0, places)
    def _(place):
        @pl.when(first[place] < 0)
        def _():
            place_of(place)[...] = jnp.zeros((size, size), BF16)

    def await_tile(position):
        pltpu.make_async_copy(
            tiles.at[position], extra.at[position], tile_sem.at[position]
        ).wait()

    for row in range(RT):
        @pl.loop(row * col_tiles, (row + 1) * col_tiles)
        def _(place):
            @pl.when(first[place] >= 0)
            def _():
                await_tile(first[place])

                @pl.when(others[place] >= 0)
                def _():
                    spot = place_of(place)
                    total[...] = spot[...].astype(F32)

                    def add(position):
                        await_tile(position)
                        total[...] += extra[position].astype(F32)
                        return following[position]

                    lax.while_loop(lambda position: position >= 0, add, others[place])
                    spot[...] = total[...].astype(BF16)

        rows = pl.ds(row * size, size)
        pltpu.make_async_copy(dense.at[rows], block.at[rows], out_sem.at[row]).start()
        if row == 0:
            feat_copy.wait()
        partial[rows, :] = jnp.dot(
            dense[rows, :], source[...], preferred_element_type=F32
        ).astype(BF16)

    for row in range(RT):
        rows = pl.ds(row * size, size)
        pltpu.make_async_copy(dense.at[rows], block.at[rows], out_sem.at[row]).wait()


def block_product(tiles, slots, count, feats):
    number, size, _ = tiles.shape
    window, width = feats.shape
    places = RT * window // size
    return pl.pallas_call(
        block_kernel,
        out_shape=(
            jax.ShapeDtypeStruct((RT * size, window), BF16),
            jax.ShapeDtypeStruct((RT * size, width), BF16),
        ),
        in_specs=[
            pl.BlockSpec(memory_space=pltpu.SMEM),
            pl.BlockSpec(memory_space=pltpu.SMEM),
            pl.BlockSpec(memory_space=pl.ANY),
            pl.BlockSpec(memory_space=pl.ANY),
        ],
        out_specs=(pl.BlockSpec(memory_space=pl.ANY), pl.BlockSpec(memory_space=pltpu.VMEM)),
        scratch_shapes=[
            pltpu.VMEM((RT * size, window), BF16),
            pltpu.VMEM((number, size, size), BF16),
            pltpu.VMEM((window, width), BF16),
            pltpu.VMEM((size, size), F32),
            pltpu.SMEM((places,), jnp.int32),
            pltpu.SMEM((places,), jnp.int32),
            pltpu.SMEM((number,), jnp.int32),
            pltpu.SemaphoreType.DMA((number,)),
            pltpu.SemaphoreType.DMA,
            pltpu.SemaphoreType.DMA((RT,)),
        ],
        compiler_params=pltpu.CompilerParams(vmem_limit_bytes=40 * 1024 * 1024),
    )(slots, count, tiles, feats)


def remote(src, dst, send_sem, recv_sem, device):
    return pltpu.make_async_remote_copy(
        src_ref=src, dst_ref=dst, send_sem=send_sem, recv_sem=recv_sem,
        device_id=device, device_id_type=MESH,
    )


def exchange_kernel(n_row, n_col, scale, block, partial, weight, out_grad,
                    activated, weight_grad, window_grad,
                    dense, core_in, pair_out, pair_in, grads, cross_out, cross_in,
                    chain_out, chain_in, total, ready, local, piece_in, piece, step_in, whole,
                    dense_sem, core_sem, pair_sem, own_sem, far_sem, pass_sem, cross_sem,
                    chain_sem, piece_sem, step_sem, whole_sem):
    n_z, n_y = n_row // 2, n_col // 2
    row, col = lax.axis_index("row"), lax.axis_index("col")
    z, x = row // 2, row % 2
    y, core = col // 2, col % 2
    share = out_grad.shape[0]
    span = window_grad.shape[0]
    width = weight.shape[0]
    depth = width // n_col
    steps = n_row.bit_length() - 1

    dense_copy = pltpu.make_async_copy(block, dense, dense_sem)
    dense_copy.start()

    sibling = (row, y * 2 + 1 - core)
    mirror = (z * 2 + 1 - x, col)
    col_peers = [(row, (col + d) % n_col) for d in range(1, n_col)]
    swaps = []
    for s in range(steps):
        bit = 1 << s
        swaps.append((row + bit - row // bit % 2 * 2 * bit, col))
    ring = [((row + 2) % n_row, col), ((row + n_row - 2) % n_row, col)]

    barrier = pltpu.get_barrier_semaphore()
    greeted = col_peers + swaps + ring
    for device in greeted:
        pl.semaphore_signal(barrier, inc=1, device_id=device, device_id_type=MESH)
    pl.semaphore_wait(barrier, len(greeted))

    started = []

    def send(copy):
        copy.start()
        started.append(copy)

    def rows_of(index, length):
        if isinstance(index, int):
            return pl.ds(index * length, length)
        return pl.ds(pl.multiple_of(index * length, length), length)

    core_copies = []
    for d in list(range(1, n_y)) + [0]:
        owner = (y + d) % n_y * 2 + 1 - core
        copy = remote(partial.at[rows_of(owner, share)], core_in.at[d],
                      core_sem.at[0, d], core_sem.at[1, d], sibling)
        send(copy)
        core_copies.append(copy)
    pair_copies = []
    for d in range(1, n_y):
        core_copies[d - 1].wait_recv()
        owner = (y + d) % n_y * 2 + core
        pair_out[d - 1] = (
            partial[rows_of(owner, share), :].astype(F32) + core_in[d].astype(F32)
        ).astype(BF16)
        copy = remote(pair_out.at[d - 1], pair_in.at[d - 1],
                      pair_sem.at[0, d - 1], pair_sem.at[1, d - 1], (row, owner))
        send(copy)
        pair_copies.append(copy)
    core_copies[-1].wait_recv()
    sums = partial[rows_of(col, share), :].astype(F32) + core_in[0].astype(F32)
    for d in range(1, n_y):
        pair_copies[d - 1].wait_recv()
        sums = sums + pair_in[d - 1].astype(F32)
    aggregated = sums.astype(BF16)

    pre_act = jnp.dot(aggregated, weight[...], preferred_element_type=F32)
    sigmoid_pre = jax.nn.sigmoid(pre_act)
    grad_pre = (
        out_grad[...].astype(F32) * sigmoid_pre * (1.0 + pre_act * (1.0 - sigmoid_pre))
    ).astype(BF16)
    grads[rows_of(col, share), :] = lax.dot_general(
        grad_pre, weight[...], (((1,), (1,)), ((), ())), preferred_element_type=F32
    ).astype(BF16)

    mine = grads.at[rows_of(col, share)]
    far_copies = []
    for d in range(1, n_y):
        copy = remote(mine, mine, far_sem.at[0, d - 1], far_sem.at[1, d - 1],
                      (row, (y + d) % n_y * 2 + core))
        send(copy)
        far_copies.append(copy)
    own_copy = remote(mine, mine, own_sem.at[0], own_sem.at[1], sibling)
    send(own_copy)

    activated[...] = (pre_act * sigmoid_pre).astype(BF16)
    local[...] = lax.dot_general(
        aggregated, grad_pre, (((0,), (0,)), ((), ())), preferred_element_type=F32
    )
    piece_copies = []
    for d in range(1, n_col):
        copy = remote(local.at[rows_of((col + d) % n_col, depth)], piece_in.at[d - 1],
                      piece_sem.at[0, d - 1], piece_sem.at[1, d - 1], col_peers[d - 1])
        send(copy)
        piece_copies.append(copy)

    pass_copies = []
    for d in range(1, n_y):
        far_copies[d - 1].wait_recv()
        got = grads.at[rows_of((y + n_y - d) % n_y * 2 + core, share)]
        copy = remote(got, got, pass_sem.at[0, d - 1], pass_sem.at[1, d - 1], sibling)
        send(copy)
        pass_copies.append(copy)
    own_copy.wait_recv()
    for copy in pass_copies:
        copy.wait_recv()
    dense_copy.wait()

    def columns_product(index, length):
        return lax.dot_general(
            dense[:, rows_of(index, length)], grads[...],
            (((0,), (0,)), ((), ())), preferred_element_type=F32,
        )

    narrow = span % LANES != 0
    if narrow:
        for tile in range(dense.shape[1] // width):
            ready[rows_of(tile, width), :] = columns_product(tile, width)

    def product(owner):
        if narrow:
            return ready[rows_of(owner, span), :]
        return columns_product(owner, span)

    high = (2 * z >= n_z).astype(jnp.int32)
    low_z = z + high * (n_z - 1 - 2 * z)

    def order(i):
        lead = n_z - 1 - 2 * low_z
        m = i - lead
        early = (m < 0).astype(jnp.int32)
        odd = jnp.abs(m) % 2
        late = (1 - odd) * (m // 2) + odd * (2 * low_z - m // 2)
        at = early * (n_z - 1 - i) + (1 - early) * late
        return at + high * (n_z - 1 - 2 * at)

    def cross_copy(at):
        return remote(cross_out.at[at], cross_in.at[at],
                      cross_sem.at[0, at], cross_sem.at[1, at], mirror)

    for i in range(n_z):
        at = order(i)
        cross_out[at] = product(at * 2 + 1 - x).astype(BF16)
        send(cross_copy(at))

    def swap_copy(s):
        return remote(piece.at[s], step_in.at[s], step_sem.at[0, s], step_sem.at[1, s], swaps[s])

    swap_copies, whole_copies = [], []

    def next_swap(s):
        if s == 0:
            added = local[rows_of(col, depth), :]
            for copy in piece_copies:
                copy.wait_recv()
            for d in range(1, n_col):
                added = added + piece_in[d - 1]
        elif s <= steps:
            swap_copies[s - 1].wait_recv()
            added = piece[s - 1] + step_in[s - 1]
        if s < steps:
            piece[s] = added
            copy = swap_copy(s)
            send(copy)
            swap_copies.append(copy)
        elif s == steps:
            spot = whole.at[rows_of(col, depth)]
            spot[...] = added * scale
            for d in range(1, n_col):
                copy = remote(spot, spot, whole_sem.at[0, d - 1], whole_sem.at[1, d - 1],
                              col_peers[d - 1])
                send(copy)
                whole_copies.append(copy)

    def chain_copy(at):
        up = (at > z).astype(jnp.int32)
        return remote(chain_out.at[at], chain_in.at[up, at],
                      chain_sem.at[0, up, at], chain_sem.at[1, up, at],
                      (row + 4 * up - 2, col))

    def await_chain(up, at):
        remote(chain_out.at[at], chain_in.at[up, at], chain_sem.at[0, up, at],
               chain_sem.at[1, up, at], mirror).wait_recv()
        total[...] += chain_in[up, at].astype(F32)

    next_swap(0)
    for i in range(n_z):
        at = order(i)
        total[...] = product(at * 2 + x)
        cross_copy(at).wait_recv()
        total[...] += cross_in[at].astype(F32)

        @pl.when(jnp.logical_and(z > 0, at >= z))
        def _():
            await_chain(1, at)

        @pl.when(jnp.logical_and(z < n_z - 1, at <= z))
        def _():
            await_chain(0, at)

        if i < n_z - 1:
            chain_out[at] = total[...].astype(BF16)
            chain_copy(at).start()
        else:
            window_grad[...] = total[...].astype(BF16)
        next_swap(i + 1)
    for s in range(n_z + 1, steps + 1):
        next_swap(s)
    for copy in whole_copies:
        copy.wait_recv()
    weight_grad[...] = whole[...]
    for copy in started:
        copy.wait_send()
    for i in range(n_z - 1):
        chain_copy(order(i)).wait_send()


def exchange(n_row, n_col, block, partial, weight, out_grad):
    rows, window = block.shape
    width = weight.shape[0]
    share = out_grad.shape[0]
    span = window // n_row
    n_z, n_y = n_row // 2, n_col // 2
    depth = width // n_col
    steps = n_row.bit_length() - 1
    dma = pltpu.SemaphoreType.DMA
    vmem = pl.BlockSpec(memory_space=pltpu.VMEM)
    return pl.pallas_call(
        functools.partial(exchange_kernel, n_row, n_col, 1.0 / math.sqrt(rows * n_row)),
        out_shape=(
            jax.ShapeDtypeStruct((share, width), BF16),
            jax.ShapeDtypeStruct((width, width), F32),
            jax.ShapeDtypeStruct((span, width), BF16),
        ),
        in_specs=[pl.BlockSpec(memory_space=pl.ANY), vmem, vmem, vmem],
        out_specs=(vmem, vmem, vmem),
        scratch_shapes=[
            pltpu.VMEM((rows, window), BF16),
            pltpu.VMEM((n_y, share, width), BF16),
            pltpu.VMEM((n_y - 1, share, width), BF16),
            pltpu.VMEM((n_y - 1, share, width), BF16),
            pltpu.VMEM((rows, width), BF16),
            pltpu.VMEM((n_z, span, width), BF16),
            pltpu.VMEM((n_z, span, width), BF16),
            pltpu.VMEM((n_z, span, width), BF16),
            pltpu.VMEM((2, n_z, span, width), BF16),
            pltpu.VMEM((span, width), F32),
            pltpu.VMEM((window if span % LANES else 8, width), F32),
            pltpu.VMEM((width, width), F32),
            pltpu.VMEM((n_col - 1, depth, width), F32),
            pltpu.VMEM((steps, depth, width), F32),
            pltpu.VMEM((steps, depth, width), F32),
            pltpu.VMEM((width, width), F32),
            dma,
            dma((2, n_y)),
            dma((2, n_y - 1)),
            dma((2,)),
            dma((2, n_y - 1)),
            dma((2, n_y - 1)),
            dma((2, n_z)),
            dma((2, 2, n_z)),
            dma((2, n_col - 1)),
            dma((2, steps)),
            dma((2, n_col - 1)),
        ],
        compiler_params=pltpu.CompilerParams(
            collective_id=0, has_side_effects=True, vmem_limit_bytes=40 * 1024 * 1024
        ),
    )(block, partial, weight, out_grad)


def on_device(n_row, n_col, tiles, tile_slot, tile_count, feats, weight, out_grad):
    block, partial = block_product(tiles[0], tile_slot[0], tile_count[0], feats)
    activated, weight_grad, window_grad = exchange(
        n_row, n_col, block, partial, weight, out_grad
    )
    return activated, weight_grad, window_grad[None]


def solution(mesh):
    placed = (
        P("row", "col", None, None),
        P("row", "col"),
        P("row", "col"),
        P("col", None),
        P(),
        P(("row", "col"), None),
    )
    return jax.shard_map(
        functools.partial(on_device, mesh.shape["row"], mesh.shape["col"]),
        mesh=mesh,
        in_specs=placed,
        out_specs=(P(("row", "col"), None), P(), P("col", "row", None)),
        check_vma=False,
    )
```

```python
import functools
import math

import jax
import jax.numpy as jnp
from jax import lax
from jax.experimental import pallas as pl
from jax.experimental.pallas import tpu as pltpu
from jax.sharding import PartitionSpec as P

RT = 4
LANES = 128
PARTS = 2
MESH = pl.DeviceIdType.MESH
F32 = jnp.float32
BF16 = jnp.bfloat16


def block_kernel(slot_list, live_count, tiles, feats, block, partial, extra, source, total,
                 slots, count, first, others, following, list_sem, tile_sem, feat_sem):
    size = tiles.shape[1]
    col_tiles = feats.shape[0] // size
    places = RT * col_tiles

    list_copies = [
        pltpu.make_async_copy(slot_list, slots, list_sem.at[0]),
        pltpu.make_async_copy(live_count, count, list_sem.at[1]),
    ]
    for copy in list_copies:
        copy.start()
    feat_copy = pltpu.make_async_copy(feats, source, feat_sem)
    feat_copy.start()

    def place_of(slot):
        row = pl.multiple_of(slot // col_tiles * size, size)
        column = pl.multiple_of(slot % col_tiles * size, size)
        return block.at[pl.ds(row, size), pl.ds(column, size)]

    for place in range(places):
        first[place] = -1
        others[place] = -1
    for copy in list_copies:
        copy.wait()
    live = count[0, 0]

    @pl.loop(0, live)
    def _(position):
        slot = slots[0, position]
        taken = first[slot] >= 0

        @pl.when(jnp.logical_not(taken))
        def _():
            first[slot] = position
            pltpu.make_async_copy(tiles.at[position], place_of(slot), tile_sem.at[position]).start()

        @pl.when(taken)
        def _():
            following[position] = others[slot]
            others[slot] = position
            pltpu.make_async_copy(
                tiles.at[position], extra.at[position], tile_sem.at[position]
            ).start()

    @pl.loop(0, places)
    def _(place):
        @pl.when(first[place] < 0)
        def _():
            place_of(place)[...] = jnp.zeros((size, size), BF16)

    def await_tile(position):
        pltpu.make_async_copy(
            tiles.at[position], extra.at[position], tile_sem.at[position]
        ).wait()

    for row in range(RT):
        @pl.loop(row * col_tiles, (row + 1) * col_tiles)
        def _(place):
            @pl.when(first[place] >= 0)
            def _():
                await_tile(first[place])

                @pl.when(others[place] >= 0)
                def _():
                    spot = place_of(place)
                    total[...] = spot[...].astype(F32)

                    def add(position):
                        await_tile(position)
                        total[...] += extra[position].astype(F32)
                        return following[position]

                    lax.while_loop(lambda position: position >= 0, add, others[place])
                    spot[...] = total[...].astype(BF16)

        rows = pl.ds(row * size, size)
        if row == 0:
            feat_copy.wait()
        partial[rows, :] = jnp.dot(
            block[rows, :], source[...], preferred_element_type=F32
        ).astype(BF16)


def block_product(tiles, slots, count, feats):
    number, size, _ = tiles.shape
    window, width = feats.shape
    places = RT * window // size
    hbm = pl.BlockSpec(memory_space=pltpu.HBM)
    vmem = pl.BlockSpec(memory_space=pltpu.VMEM)
    return pl.pallas_call(
        block_kernel,
        out_shape=(
            jax.ShapeDtypeStruct((RT * size, window), BF16),
            jax.ShapeDtypeStruct((RT * size, width), BF16),
        ),
        in_specs=[hbm, hbm, hbm, hbm],
        out_specs=(vmem, vmem),
        scratch_shapes=[
            pltpu.VMEM((number, size, size), BF16),
            pltpu.VMEM((window, width), BF16),
            pltpu.VMEM((size, size), F32),
            pltpu.SMEM(slots.shape, jnp.int32),
            pltpu.SMEM(count.shape, jnp.int32),
            pltpu.SMEM((places,), jnp.int32),
            pltpu.SMEM((places,), jnp.int32),
            pltpu.SMEM((number,), jnp.int32),
            pltpu.SemaphoreType.DMA((2,)),
            pltpu.SemaphoreType.DMA((number,)),
            pltpu.SemaphoreType.DMA,
        ],
        compiler_params=pltpu.CompilerParams(vmem_limit_bytes=24 * 1024 * 1024),
    )(slots, count, tiles, feats)


def publish_kernel(*refs):
    number = len(refs) // 2
    sem = refs[-1]
    copies = [
        pltpu.make_async_copy(refs[i], refs[number + i], sem.at[i]) for i in range(number)
    ]
    for copy in copies:
        copy.start()
    for copy in copies:
        copy.wait()


def publish(*results):
    return pl.pallas_call(
        publish_kernel,
        out_shape=tuple(jax.ShapeDtypeStruct(r.shape, r.dtype) for r in results),
        in_specs=[pl.BlockSpec(memory_space=pltpu.VMEM)] * len(results),
        out_specs=tuple(pl.BlockSpec(memory_space=pltpu.HBM) for _ in results),
        scratch_shapes=[pltpu.SemaphoreType.DMA((len(results),))],
    )(*results)


def remote(src, dst, send_sem, recv_sem, device):
    return pltpu.make_async_remote_copy(
        src_ref=src, dst_ref=dst, send_sem=send_sem, recv_sem=recv_sem,
        device_id=device, device_id_type=MESH,
    )


def exchange_kernel(n_row, n_col, scale, block, partial, weight, out_grad,
                    activated, weight_grad, window_grad,
                    core_in, pair_out, pair_in, grads, grads_wide, cross_out, cross_in,
                    chain_out, chain_in, total, ready, local, piece_in, piece, step_in, whole,
                    core_sem, pair_sem, own_sem, far_sem, pass_sem, cross_sem,
                    chain_sem, piece_sem, step_sem, whole_sem):
    n_z, n_y = n_row // 2, n_col // 2
    row, col = lax.axis_index("row"), lax.axis_index("col")
    z, x = row // 2, row % 2
    y, core = col // 2, col % 2
    share = out_grad.shape[0]
    span = window_grad.shape[0]
    width = weight.shape[0]
    depth = width // n_col
    steps = n_row.bit_length() - 1
    cut = share // PARTS

    sibling = (row, y * 2 + 1 - core)
    mirror = (z * 2 + 1 - x, col)
    col_peers = [(row, (col + d) % n_col) for d in range(1, n_col)]
    swaps = []
    for s in list(range(1, steps)) + [0]:
        bit = 1 << s
        swaps.append((row + bit - row // bit % 2 * 2 * bit, col))
    ring = [((row + 2) % n_row, col), ((row + n_row - 2) % n_row, col)]

    barrier = pltpu.get_barrier_semaphore()
    greeted = col_peers + swaps + ring
    for device in greeted:
        pl.semaphore_signal(barrier, inc=1, device_id=device, device_id_type=MESH)
    pl.semaphore_wait(barrier, len(greeted))

    started = []

    def send(*args):
        copy = remote(*args)
        copy.start()
        started.append(copy)
        return copy

    def rows_of(index, length):
        if isinstance(index, int):
            return pl.ds(index * length, length)
        return pl.ds(pl.multiple_of(index * length, length), length)

    def part_of(owner, part):
        return rows_of(owner * PARTS + part, cut)

    core_copies = {}
    for d in list(range(1, n_y)) + [0]:
        for part in range(PARTS):
            owner = (y + d) % n_y * 2 + 1 - core
            core_copies[d, part] = send(
                partial.at[part_of(owner, part)], core_in.at[d, part],
                core_sem.at[0, d, part], core_sem.at[1, d, part], sibling)
    pair_copies = {}
    for part in range(PARTS):
        for d in range(1, n_y):
            core_copies[d, part].wait_recv()
            owner = (y + d) % n_y * 2 + core
            pair_out[d - 1, part] = (
                partial[part_of(owner, part), :].astype(F32) + core_in[d, part].astype(F32)
            ).astype(BF16)
            pair_copies[d, part] = send(
                pair_out.at[d - 1, part], pair_in.at[d - 1, part],
                pair_sem.at[0, d - 1, part], pair_sem.at[1, d - 1, part], (row, owner))

    far_copies, own_copies = {}, []
    for part in range(PARTS):
        core_copies[0, part].wait_recv()
        sums = partial[part_of(col, part), :].astype(F32) + core_in[0, part].astype(F32)
        for d in range(1, n_y):
            pair_copies[d, part].wait_recv()
            sums = sums + pair_in[d - 1, part].astype(F32)
        aggregated = sums.astype(BF16)
        pre_act = jnp.dot(aggregated, weight[...], preferred_element_type=F32)
        sigmoid_pre = jax.nn.sigmoid(pre_act)
        rows = pl.ds(part * cut, cut)
        grad_pre = (
            out_grad[rows, :].astype(F32) * sigmoid_pre * (1.0 + pre_act * (1.0 - sigmoid_pre))
        ).astype(BF16)
        grads[col, part] = lax.dot_general(
            weight[...], grad_pre, (((1,), (1,)), ((), ())), preferred_element_type=F32
        ).astype(BF16)
        mine = grads.at[col, part]
        for d in range(1, n_y):
            far_copies[d, part] = send(
                mine, mine, far_sem.at[0, d - 1, part], far_sem.at[1, d - 1, part],
                (row, (y + d) % n_y * 2 + core))
        own_copies.append(send(mine, mine, own_sem.at[0, part], own_sem.at[1, part], sibling))
        activated[rows, :] = (pre_act * sigmoid_pre).astype(BF16)
        outer = lax.dot_general(
            aggregated, grad_pre, (((0,), (0,)), ((), ())), preferred_element_type=F32
        )
        if part == 0:
            local[...] = outer
        else:
            local[...] += outer

    piece_copies = []
    for d in range(1, n_col):
        piece_copies.append(send(
            local.at[rows_of((col + d) % n_col, depth)], piece_in.at[d - 1],
            piece_sem.at[0, d - 1], piece_sem.at[1, d - 1], col_peers[d - 1]))

    pass_copies = []
    for part in range(PARTS):
        for d in range(1, n_y):
            far_copies[d, part].wait_recv()
            got = grads.at[(y + n_y - d) % n_y * 2 + core, part]
            pass_copies.append(send(
                got, got, pass_sem.at[0, d - 1, part], pass_sem.at[1, d - 1, part], sibling))
    for copy in own_copies + pass_copies:
        copy.wait_recv()
    for owner in range(n_col):
        for part in range(PARTS):
            grads_wide[:, part_of(owner, part)] = grads[owner, part]

    def columns_product(index, length):
        return jnp.dot(
            grads_wide[...], block[:, rows_of(index, length)], preferred_element_type=F32
        )

    narrow = span % LANES != 0
    if narrow:
        for tile in range(block.shape[1] // width):
            ready[rows_of(tile, width), :] = columns_product(tile, width).T

    def product(owner):
        if narrow:
            return ready[rows_of(owner, span), :]
        return columns_product(owner, span)

    high = (2 * z >= n_z).astype(jnp.int32)
    low_z = z + high * (n_z - 1 - 2 * z)

    def order(i):
        lead = n_z - 1 - 2 * low_z
        m = i - lead
        early = (m < 0).astype(jnp.int32)
        odd = jnp.abs(m) % 2
        late = (1 - odd) * (m // 2) + odd * (2 * low_z - m // 2)
        at = early * (n_z - 1 - i) + (1 - early) * late
        return at + high * (n_z - 1 - 2 * at)

    slab = total.shape[0] // PARTS

    def cross_copy(at, part):
        rows = pl.ds(part * slab, slab)
        return (cross_out.at[at, rows], cross_in.at[at, rows],
                cross_sem.at[0, at, part], cross_sem.at[1, at, part], mirror)

    for i in range(n_z):
        at = order(i)
        cross_out[at] = product(at * 2 + 1 - x).astype(BF16)
        for part in range(PARTS):
            send(*cross_copy(at, part))

    swap_copies, whole_copies = [], []

    def next_swap(s):
        if s == 0:
            added = local[rows_of(col, depth), :]
            for copy in piece_copies:
                copy.wait_recv()
            for d in range(1, n_col):
                added = added + piece_in[d - 1]
        elif s <= steps:
            swap_copies[s - 1].wait_recv()
            added = piece[s - 1] + step_in[s - 1]
        if s < steps:
            piece[s] = added
            swap_copies.append(send(
                piece.at[s], step_in.at[s], step_sem.at[0, s], step_sem.at[1, s], swaps[s]))
        elif s == steps:
            spot = whole.at[rows_of(col, depth)]
            spot[...] = added * scale
            for d in range(1, n_col):
                whole_copies.append(send(
                    spot, spot, whole_sem.at[0, d - 1], whole_sem.at[1, d - 1],
                    col_peers[d - 1]))

    def chain_copy(at, part):
        rows = pl.ds(part * slab, slab)
        up = (at > z).astype(jnp.int32)
        return remote(chain_out.at[at, rows], chain_in.at[up, at, rows],
                      chain_sem.at[0, up, at, part], chain_sem.at[1, up, at, part],
                      (row + 4 * up - 2, col))

    def await_chain(up, at, part):
        rows = pl.ds(part * slab, slab)
        remote(chain_out.at[at, rows], chain_in.at[up, at, rows],
               chain_sem.at[0, up, at, part], chain_sem.at[1, up, at, part], mirror).wait_recv()
        total[rows, :] += chain_in[up, at, rows, :].astype(F32)

    next_swap(0)
    for i in range(n_z):
        at = order(i)
        total[...] = product(at * 2 + x)
        for part in range(PARTS):
            rows = pl.ds(part * slab, slab)
            remote(*cross_copy(at, part)).wait_recv()
            total[rows, :] += cross_in[at, rows, :].astype(F32)

            @pl.when(jnp.logical_and(z > 0, at >= z))
            def _():
                await_chain(1, at, part)

            @pl.when(jnp.logical_and(z < n_z - 1, at <= z))
            def _():
                await_chain(0, at, part)

            if i < n_z - 1:
                chain_out[at, rows, :] = total[rows, :].astype(BF16)
                chain_copy(at, part).start()
        if i == n_z - 1:
            result = total[...] if narrow else total[...].T
            window_grad[...] = result.astype(BF16)
        next_swap(i + 1)
    for s in range(n_z + 1, steps + 1):
        next_swap(s)
    for copy in whole_copies:
        copy.wait_recv()
    weight_grad[...] = whole[...]
    for copy in started:
        copy.wait_send()
    for i in range(n_z - 1):
        for part in range(PARTS):
            chain_copy(order(i), part).wait_send()


def exchange(n_row, n_col, block, partial, weight, out_grad):
    rows, window = block.shape
    width = weight.shape[0]
    share = out_grad.shape[0]
    span = window // n_row
    n_z, n_y = n_row // 2, n_col // 2
    depth = width // n_col
    steps = n_row.bit_length() - 1
    cut = share // PARTS
    narrow = span % LANES != 0
    chunk = (span, width) if narrow else (width, span)
    dma = pltpu.SemaphoreType.DMA
    vmem = pl.BlockSpec(memory_space=pltpu.VMEM)
    return pl.pallas_call(
        functools.partial(exchange_kernel, n_row, n_col, 1.0 / math.sqrt(rows * n_row)),
        out_shape=(
            jax.ShapeDtypeStruct((share, width), BF16),
            jax.ShapeDtypeStruct((width, width), F32),
            jax.ShapeDtypeStruct((span, width), BF16),
        ),
        in_specs=[vmem, vmem, vmem, vmem],
        out_specs=(vmem, vmem, vmem),
        scratch_shapes=[
            pltpu.VMEM((n_y, PARTS, cut, width), BF16),
            pltpu.VMEM((n_y - 1, PARTS, cut, width), BF16),
            pltpu.VMEM((n_y - 1, PARTS, cut, width), BF16),
            pltpu.VMEM((n_col, PARTS, width, cut), BF16),
            pltpu.VMEM((width, rows), BF16),
            pltpu.VMEM((n_z, *chunk), BF16),
            pltpu.VMEM((n_z, *chunk), BF16),
            pltpu.VMEM((n_z, *chunk), BF16),
            pltpu.VMEM((2, n_z, *chunk), BF16),
            pltpu.VMEM(chunk, F32),
            pltpu.VMEM((window if narrow else 8, width), F32),
            pltpu.VMEM((width, width), F32),
            pltpu.VMEM((n_col - 1, depth, width), F32),
            pltpu.VMEM((steps, depth, width), F32),
            pltpu.VMEM((steps, depth, width), F32),
            pltpu.VMEM((width, width), F32),
            dma((2, n_y, PARTS)),
            dma((2, n_y - 1, PARTS)),
            dma((2, PARTS)),
            dma((2, n_y - 1, PARTS)),
            dma((2, n_y - 1, PARTS)),
            dma((2, n_z, PARTS)),
            dma((2, 2, n_z, PARTS)),
            dma((2, n_col - 1)),
            dma((2, steps)),
            dma((2, n_col - 1)),
        ],
        compiler_params=pltpu.CompilerParams(
            collective_id=0, has_side_effects=True, vmem_limit_bytes=40 * 1024 * 1024
        ),
    )(block, partial, weight, out_grad)


def on_device(n_row, n_col, tiles, tile_slot, tile_count, feats, weight, out_grad):
    held = [
        pltpu.with_memory_space_constraint(array, pltpu.HBM)
        for array in (tiles[0], tile_slot, feats)
    ]
    block, partial = block_product(held[0], held[1], tile_count, held[2])
    activated, weight_grad, window_grad = exchange(
        n_row, n_col, block, partial, weight, out_grad
    )
    activated, weight_grad, window_grad = publish(activated, weight_grad, window_grad)
    return activated, weight_grad, window_grad[None]


def solution(mesh):
    placed = (
        P("row", "col", None, None),
        P("row", "col"),
        P("row", "col"),
        P("col", None),
        P(),
        P(("row", "col"), None),
    )
    return jax.shard_map(
        functools.partial(on_device, mesh.shape["row"], mesh.shape["col"]),
        mesh=mesh,
        in_specs=placed,
        out_specs=(P(("row", "col"), None), P(), P("col", "row", None)),
        check_vma=False,
    )
```

```python
import functools
import math

import jax
import jax.numpy as jnp
from jax import lax
from jax.experimental import pallas as pl
from jax.experimental.pallas import tpu as pltpu
from jax.sharding import PartitionSpec as P

RT = 4
LANES = 128
PARTS = 2
MESH = pl.DeviceIdType.MESH
F32 = jnp.float32
BF16 = jnp.bfloat16


def block_kernel(slot_list, live_count, tiles, feats, block, partial, extra, source, total,
                 slots, count, first, others, following, list_sem, tile_sem, feat_sem):
    size = tiles.shape[1]
    col_tiles = feats.shape[0] // size
    places = RT * col_tiles

    list_copies = [
        pltpu.make_async_copy(slot_list, slots, list_sem.at[0]),
        pltpu.make_async_copy(live_count, count, list_sem.at[1]),
    ]
    for copy in list_copies:
        copy.start()
    feat_copy = pltpu.make_async_copy(feats, source, feat_sem)
    feat_copy.start()

    def place_of(slot):
        row = pl.multiple_of(slot // col_tiles * size, size)
        column = pl.multiple_of(slot % col_tiles * size, size)
        return block.at[pl.ds(row, size), pl.ds(column, size)]

    for place in range(places):
        first[place] = -1
        others[place] = -1
    for copy in list_copies:
        copy.wait()
    live = count[0, 0]

    @pl.loop(0, live)
    def _(position):
        slot = slots[0, position]
        taken = first[slot] >= 0

        @pl.when(jnp.logical_not(taken))
        def _():
            first[slot] = position
            pltpu.make_async_copy(tiles.at[position], place_of(slot), tile_sem.at[position]).start()

        @pl.when(taken)
        def _():
            following[position] = others[slot]
            others[slot] = position
            pltpu.make_async_copy(
                tiles.at[position], extra.at[position], tile_sem.at[position]
            ).start()

    @pl.loop(0, places)
    def _(place):
        @pl.when(first[place] < 0)
        def _():
            place_of(place)[...] = jnp.zeros((size, size), BF16)

    def await_tile(position):
        pltpu.make_async_copy(
            tiles.at[position], extra.at[position], tile_sem.at[position]
        ).wait()

    for row in range(RT):
        @pl.loop(row * col_tiles, (row + 1) * col_tiles)
        def _(place):
            @pl.when(first[place] >= 0)
            def _():
                await_tile(first[place])

                @pl.when(others[place] >= 0)
                def _():
                    spot = place_of(place)
                    total[...] = spot[...].astype(F32)

                    def add(position):
                        await_tile(position)
                        total[...] += extra[position].astype(F32)
                        return following[position]

                    lax.while_loop(lambda position: position >= 0, add, others[place])
                    spot[...] = total[...].astype(BF16)

        if row % 2 == 1:
            if row == 1:
                feat_copy.wait()
            rows = pl.ds((row - 1) * size, 2 * size)
            partial[rows, :] = jnp.dot(
                block[rows, :], source[...], preferred_element_type=F32
            ).astype(BF16)


def block_product(tiles, slots, count, feats):
    number, size, _ = tiles.shape
    window, width = feats.shape
    places = RT * window // size
    hbm = pl.BlockSpec(memory_space=pltpu.HBM)
    vmem = pl.BlockSpec(memory_space=pltpu.VMEM)
    return pl.pallas_call(
        block_kernel,
        out_shape=(
            jax.ShapeDtypeStruct((RT * size, window), BF16),
            jax.ShapeDtypeStruct((RT * size, width), BF16),
        ),
        in_specs=[hbm, hbm, hbm, hbm],
        out_specs=(vmem, vmem),
        scratch_shapes=[
            pltpu.VMEM((number, size, size), BF16),
            pltpu.VMEM((window, width), BF16),
            pltpu.VMEM((size, size), F32),
            pltpu.SMEM(slots.shape, jnp.int32),
            pltpu.SMEM(count.shape, jnp.int32),
            pltpu.SMEM((places,), jnp.int32),
            pltpu.SMEM((places,), jnp.int32),
            pltpu.SMEM((number,), jnp.int32),
            pltpu.SemaphoreType.DMA((2,)),
            pltpu.SemaphoreType.DMA((number,)),
            pltpu.SemaphoreType.DMA,
        ],
        compiler_params=pltpu.CompilerParams(vmem_limit_bytes=24 * 1024 * 1024),
    )(slots, count, tiles, feats)


def remote(src, dst, send_sem, recv_sem, device):
    return pltpu.make_async_remote_copy(
        src_ref=src, dst_ref=dst, send_sem=send_sem, recv_sem=recv_sem,
        device_id=device, device_id_type=MESH,
    )


def exchange_kernel(n_row, n_col, scale, block, partial, weight, out_grad,
                    activated, weight_grad, window_grad,
                    core_in, pair_out, pair_in, grads, grads_wide, cross_out, cross_in,
                    chain_out, chain_in, total, ready, local, local_out, piece_in, piece, step_in, whole,
                    core_sem, pair_sem, own_sem, far_sem, pass_sem, cross_sem,
                    chain_sem, piece_sem, step_sem, whole_sem):
    n_z, n_y = n_row // 2, n_col // 2
    row, col = lax.axis_index("row"), lax.axis_index("col")
    z, x = row // 2, row % 2
    y, core = col // 2, col % 2
    share = out_grad.shape[0]
    span = window_grad.shape[0]
    width = weight.shape[0]
    depth = width // n_col
    steps = n_row.bit_length() - 1
    cut = share // PARTS

    sibling = (row, y * 2 + 1 - core)
    mirror = (z * 2 + 1 - x, col)
    col_peers = [(row, (col + d) % n_col) for d in range(1, n_col)]
    swaps = []
    for s in range(steps):
        bit = 1 << s
        swaps.append((row + bit - row // bit % 2 * 2 * bit, col))
    ring = [((row + 2) % n_row, col), ((row + n_row - 2) % n_row, col)]

    barrier = pltpu.get_barrier_semaphore()
    greeted = col_peers + swaps + ring
    for device in greeted:
        pl.semaphore_signal(barrier, inc=1, device_id=device, device_id_type=MESH)
    pl.semaphore_wait(barrier, len(greeted))

    started = []

    def send(*args):
        copy = remote(*args)
        copy.start()
        started.append(copy)
        return copy

    def rows_of(index, length):
        if isinstance(index, int):
            return pl.ds(index * length, length)
        return pl.ds(pl.multiple_of(index * length, length), length)

    def part_of(owner, part):
        return rows_of(owner * PARTS + part, cut)

    core_copies = {}
    for d in list(range(1, n_y)) + [0]:
        for part in range(PARTS):
            owner = (y + d) % n_y * 2 + 1 - core
            core_copies[d, part] = send(
                partial.at[part_of(owner, part)], core_in.at[d, part],
                core_sem.at[0, d, part], core_sem.at[1, d, part], sibling)
    pair_copies = {}
    for part in range(PARTS):
        for d in range(1, n_y):
            core_copies[d, part].wait_recv()
            owner = (y + d) % n_y * 2 + core
            pair_out[d - 1, part] = (
                partial[part_of(owner, part), :].astype(F32) + core_in[d, part].astype(F32)
            ).astype(BF16)
            pair_copies[d, part] = send(
                pair_out.at[d - 1, part], pair_in.at[d - 1, part],
                pair_sem.at[0, d - 1, part], pair_sem.at[1, d - 1, part], (row, owner))

    far_copies, own_copies = {}, []
    for part in range(PARTS):
        core_copies[0, part].wait_recv()
        sums = partial[part_of(col, part), :].astype(F32) + core_in[0, part].astype(F32)
        for d in range(1, n_y):
            pair_copies[d, part].wait_recv()
            sums = sums + pair_in[d - 1, part].astype(F32)
        aggregated = sums.astype(BF16)
        pre_act = jnp.dot(aggregated, weight[...], preferred_element_type=F32)
        sigmoid_pre = jax.nn.sigmoid(pre_act)
        rows = pl.ds(part * cut, cut)
        grad_pre = (
            out_grad[rows, :].astype(F32) * sigmoid_pre * (1.0 + pre_act * (1.0 - sigmoid_pre))
        ).astype(BF16)
        grads[col, part] = lax.dot_general(
            weight[...], grad_pre, (((1,), (1,)), ((), ())), preferred_element_type=F32
        ).astype(BF16)
        mine = grads.at[col, part]
        for d in range(1, n_y):
            far_copies[d, part] = send(
                mine, mine, far_sem.at[0, d - 1, part], far_sem.at[1, d - 1, part],
                (row, (y + d) % n_y * 2 + core))
        own_copies.append(send(mine, mine, own_sem.at[0, part], own_sem.at[1, part], sibling))
        activated[rows, :] = (pre_act * sigmoid_pre).astype(BF16)
        outer = lax.dot_general(
            aggregated, grad_pre, (((0,), (0,)), ((), ())), preferred_element_type=F32
        )
        if part == 0:
            local[...] = outer
        else:
            local[...] += outer

    pass_copies = []
    for part in range(PARTS):
        for d in range(1, n_y):
            far_copies[d, part].wait_recv()
            got = grads.at[(y + n_y - d) % n_y * 2 + core, part]
            pass_copies.append(send(
                got, got, pass_sem.at[0, d - 1, part], pass_sem.at[1, d - 1, part], sibling))
    local_out[...] = local[...].astype(BF16)
    piece_copies = []
    for d in range(1, n_col):
        piece_copies.append(send(
            local_out.at[rows_of((col + d) % n_col, depth)], piece_in.at[d - 1],
            piece_sem.at[0, d - 1], piece_sem.at[1, d - 1], col_peers[d - 1]))
    for copy in own_copies + pass_copies:
        copy.wait_recv()
    for owner in range(n_col):
        for part in range(PARTS):
            grads_wide[:, part_of(owner, part)] = grads[owner, part]

    def columns_product(index, length):
        return jnp.dot(
            grads_wide[...], block[:, rows_of(index, length)], preferred_element_type=F32
        )

    narrow = span % LANES != 0
    if narrow:
        for tile in range(block.shape[1] // width):
            ready[rows_of(tile, width), :] = columns_product(tile, width).T

    def product(owner):
        if narrow:
            return ready[rows_of(owner, span), :]
        return columns_product(owner, span)

    high = (2 * z >= n_z).astype(jnp.int32)
    low_z = z + high * (n_z - 1 - 2 * z)

    def order(i):
        lead = n_z - 1 - 2 * low_z
        m = i - lead
        early = (m < 0).astype(jnp.int32)
        odd = jnp.abs(m) % 2
        late = (1 - odd) * (m // 2) + odd * (2 * low_z - m // 2)
        at = early * (n_z - 1 - i) + (1 - early) * late
        return at + high * (n_z - 1 - 2 * at)

    slab = total.shape[0] // PARTS

    def cross_copy(at, part):
        rows = pl.ds(part * slab, slab)
        return (cross_out.at[at, rows], cross_in.at[at, rows],
                cross_sem.at[0, at, part], cross_sem.at[1, at, part], mirror)

    swap_copies, whole_copies = [], []

    def next_swap(s):
        if s == 0:
            added = local[rows_of(col, depth), :]
            for copy in piece_copies:
                copy.wait_recv()
            for d in range(1, n_col):
                added = added + piece_in[d - 1].astype(F32)
        elif s <= steps:
            swap_copies[s - 1].wait_recv()
            added = piece[s - 1].astype(F32) + step_in[s - 1].astype(F32)
        if s < steps:
            piece[s] = added.astype(BF16)
            swap_copies.append(send(
                piece.at[s], step_in.at[s], step_sem.at[0, s], step_sem.at[1, s], swaps[s]))
        elif s == steps:
            spot = whole.at[rows_of(col, depth)]
            spot[...] = (added * scale).astype(BF16)
            for d in range(1, n_col):
                whole_copies.append(send(
                    spot, spot, whole_sem.at[0, d - 1], whole_sem.at[1, d - 1],
                    col_peers[d - 1]))

    def chain_copy(at, part):
        rows = pl.ds(part * slab, slab)
        up = (at > z).astype(jnp.int32)
        return remote(chain_out.at[at, rows], chain_in.at[up, at, rows],
                      chain_sem.at[0, up, at, part], chain_sem.at[1, up, at, part],
                      (row + 4 * up - 2, col))

    def await_chain(up, at, part):
        rows = pl.ds(part * slab, slab)
        remote(chain_out.at[at, rows], chain_in.at[up, at, rows],
               chain_sem.at[0, up, at, part], chain_sem.at[1, up, at, part], mirror).wait_recv()
        total[rows, :] += chain_in[up, at, rows, :].astype(F32)

    for i in range(n_z):
        at = order(i)
        cross_out[at] = product(at * 2 + 1 - x).astype(BF16)
        for part in range(PARTS):
            send(*cross_copy(at, part))
        if i == 0:
            next_swap(0)
    for i in range(n_z):
        at = order(i)
        total[...] = product(at * 2 + x)
        for part in range(PARTS):
            rows = pl.ds(part * slab, slab)
            remote(*cross_copy(at, part)).wait_recv()
            total[rows, :] += cross_in[at, rows, :].astype(F32)

            @pl.when(jnp.logical_and(z > 0, at >= z))
            def _():
                await_chain(1, at, part)

            @pl.when(jnp.logical_and(z < n_z - 1, at <= z))
            def _():
                await_chain(0, at, part)

            if i < n_z - 1:
                chain_out[at, rows, :] = total[rows, :].astype(BF16)
                chain_copy(at, part).start()
        if i == n_z - 1:
            result = total[...] if narrow else total[...].T
            window_grad[...] = result.astype(BF16)
        next_swap(i + 1)
    for s in range(n_z + 1, steps + 1):
        next_swap(s)
    for copy in whole_copies:
        copy.wait_recv()
    weight_grad[...] = whole[...].astype(F32)
    for copy in started:
        copy.wait_send()
    for i in range(n_z - 1):
        for part in range(PARTS):
            chain_copy(order(i), part).wait_send()


def exchange(n_row, n_col, block, partial, weight, out_grad):
    rows, window = block.shape
    width = weight.shape[0]
    share = out_grad.shape[0]
    span = window // n_row
    n_z, n_y = n_row // 2, n_col // 2
    depth = width // n_col
    steps = n_row.bit_length() - 1
    cut = share // PARTS
    narrow = span % LANES != 0
    chunk = (span, width) if narrow else (width, span)
    dma = pltpu.SemaphoreType.DMA
    vmem = pl.BlockSpec(memory_space=pltpu.VMEM)
    return pl.pallas_call(
        functools.partial(exchange_kernel, n_row, n_col, 1.0 / math.sqrt(rows * n_row)),
        out_shape=(
            jax.ShapeDtypeStruct((share, width), BF16),
            jax.ShapeDtypeStruct((width, width), F32),
            jax.ShapeDtypeStruct((span, width), BF16),
        ),
        in_specs=[vmem, vmem, vmem, vmem],
        out_specs=(vmem, vmem, vmem),
        scratch_shapes=[
            pltpu.VMEM((n_y, PARTS, cut, width), BF16),
            pltpu.VMEM((n_y - 1, PARTS, cut, width), BF16),
            pltpu.VMEM((n_y - 1, PARTS, cut, width), BF16),
            pltpu.VMEM((n_col, PARTS, width, cut), BF16),
            pltpu.VMEM((width, rows), BF16),
            pltpu.VMEM((n_z, *chunk), BF16),
            pltpu.VMEM((n_z, *chunk), BF16),
            pltpu.VMEM((n_z, *chunk), BF16),
            pltpu.VMEM((2, n_z, *chunk), BF16),
            pltpu.VMEM(chunk, F32),
            pltpu.VMEM((window if narrow else 8, width), F32),
            pltpu.VMEM((width, width), F32),
            pltpu.VMEM((width, width), BF16),
            pltpu.VMEM((n_col - 1, depth, width), BF16),
            pltpu.VMEM((steps, depth, width), BF16),
            pltpu.VMEM((steps, depth, width), BF16),
            pltpu.VMEM((width, width), BF16),
            dma((2, n_y, PARTS)),
            dma((2, n_y - 1, PARTS)),
            dma((2, PARTS)),
            dma((2, n_y - 1, PARTS)),
            dma((2, n_y - 1, PARTS)),
            dma((2, n_z, PARTS)),
            dma((2, 2, n_z, PARTS)),
            dma((2, n_col - 1)),
            dma((2, steps)),
            dma((2, n_col - 1)),
        ],
        compiler_params=pltpu.CompilerParams(
            collective_id=0, has_side_effects=True, vmem_limit_bytes=40 * 1024 * 1024
        ),
    )(block, partial, weight, out_grad)


def on_device(n_row, n_col, tiles, tile_slot, tile_count, feats, weight, out_grad):
    held = [
        pltpu.with_memory_space_constraint(array, pltpu.HBM)
        for array in (tiles[0], tile_slot, feats)
    ]
    block, partial = block_product(held[0], held[1], tile_count, held[2])
    activated, weight_grad, window_grad = exchange(
        n_row, n_col, block, partial, weight, out_grad
    )
    return activated, weight_grad, window_grad[None]


def solution(mesh):
    placed = (
        P("row", "col", None, None),
        P("row", "col"),
        P("row", "col"),
        P("col", None),
        P(),
        P(("row", "col"), None),
    )
    return jax.shard_map(
        functools.partial(on_device, mesh.shape["row"], mesh.shape["col"]),
        mesh=mesh,
        in_specs=placed,
        out_specs=(P(("row", "col"), None), P(), P("col", "row", None)),
        check_vma=False,
    )
```

```python
import functools
import math

import jax
import jax.numpy as jnp
from jax import lax
from jax.experimental import pallas as pl
from jax.experimental.pallas import tpu as pltpu
from jax.sharding import PartitionSpec as P

RT = 4
LANES = 128
PARTS = 2
MESH = pl.DeviceIdType.MESH
F32 = jnp.float32
BF16 = jnp.bfloat16


def block_kernel(slot_list, count, tiles, feats, block, partial, extra, source, total,
                 slots, first, others, following, list_sem, tile_sem, feat_sem):
    size = tiles.shape[1]
    col_tiles = feats.shape[0] // size
    places = RT * col_tiles

    list_copy = pltpu.make_async_copy(slot_list, slots, list_sem)
    list_copy.start()
    feat_copy = pltpu.make_async_copy(feats, source, feat_sem)
    feat_copy.start()

    def place_of(slot):
        row = pl.multiple_of(slot // col_tiles * size, size)
        column = pl.multiple_of(slot % col_tiles * size, size)
        return block.at[pl.ds(row, size), pl.ds(column, size)]

    for place in range(places):
        first[place] = -1
        others[place] = -1
    list_copy.wait()
    live = count[0, 0]

    @pl.loop(0, live)
    def _(position):
        slot = slots[0, position]
        taken = first[slot] >= 0

        @pl.when(jnp.logical_not(taken))
        def _():
            first[slot] = position
            pltpu.make_async_copy(tiles.at[position], place_of(slot), tile_sem.at[position]).start()

        @pl.when(taken)
        def _():
            following[position] = others[slot]
            others[slot] = position
            pltpu.make_async_copy(
                tiles.at[position], extra.at[position], tile_sem.at[position]
            ).start()

    @pl.loop(0, places)
    def _(place):
        @pl.when(first[place] < 0)
        def _():
            place_of(place)[...] = jnp.zeros((size, size), BF16)

    def await_tile(position):
        pltpu.make_async_copy(
            tiles.at[position], extra.at[position], tile_sem.at[position]
        ).wait()

    for row in range(RT):
        @pl.loop(row * col_tiles, (row + 1) * col_tiles)
        def _(place):
            @pl.when(first[place] >= 0)
            def _():
                await_tile(first[place])

                @pl.when(others[place] >= 0)
                def _():
                    spot = place_of(place)
                    total[...] = spot[...].astype(F32)

                    def add(position):
                        await_tile(position)
                        total[...] += extra[position].astype(F32)
                        return following[position]

                    lax.while_loop(lambda position: position >= 0, add, others[place])
                    spot[...] = total[...].astype(BF16)

        if row % 2 == 1:
            if row == 1:
                feat_copy.wait()
            rows = pl.ds((row - 1) * size, 2 * size)
            partial[rows, :] = jnp.dot(
                block[rows, :], source[...], preferred_element_type=F32
            ).astype(BF16)


def block_product(tiles, slots, count, feats):
    number, size, _ = tiles.shape
    window, width = feats.shape
    places = RT * window // size
    hbm = pl.BlockSpec(memory_space=pltpu.HBM)
    vmem = pl.BlockSpec(memory_space=pltpu.VMEM)
    return pl.pallas_call(
        block_kernel,
        out_shape=(
            jax.ShapeDtypeStruct((RT * size, window), BF16),
            jax.ShapeDtypeStruct((RT * size, width), BF16),
        ),
        in_specs=[hbm, pl.BlockSpec(memory_space=pltpu.SMEM), hbm, hbm],
        out_specs=(vmem, vmem),
        scratch_shapes=[
            pltpu.VMEM((number, size, size), BF16),
            pltpu.VMEM((window, width), BF16),
            pltpu.VMEM((size, size), F32),
            pltpu.SMEM(slots.shape, jnp.int32),
            pltpu.SMEM((places,), jnp.int32),
            pltpu.SMEM((places,), jnp.int32),
            pltpu.SMEM((number,), jnp.int32),
            pltpu.SemaphoreType.DMA,
            pltpu.SemaphoreType.DMA((number,)),
            pltpu.SemaphoreType.DMA,
        ],
        compiler_params=pltpu.CompilerParams(vmem_limit_bytes=24 * 1024 * 1024),
    )(slots, count, tiles, feats)


def publish_kernel(*refs):
    number = len(refs) // 2
    sem = refs[-1]
    copies = [
        pltpu.make_async_copy(refs[i], refs[number + i], sem.at[i]) for i in range(number)
    ]
    for copy in copies:
        copy.start()
    for copy in copies:
        copy.wait()


def publish(*results):
    held = [pltpu.with_memory_space_constraint(r, pltpu.VMEM) for r in results]
    return pl.pallas_call(
        publish_kernel,
        out_shape=tuple(jax.ShapeDtypeStruct(r.shape, r.dtype) for r in results),
        in_specs=[pl.BlockSpec(memory_space=pltpu.VMEM)] * len(results),
        out_specs=tuple(pl.BlockSpec(memory_space=pltpu.HBM) for _ in results),
        scratch_shapes=[pltpu.SemaphoreType.DMA((len(results),))],
    )(*held)


def remote(src, dst, send_sem, recv_sem, device):
    return pltpu.make_async_remote_copy(
        src_ref=src, dst_ref=dst, send_sem=send_sem, recv_sem=recv_sem,
        device_id=device, device_id_type=MESH,
    )


def slabs_of(rows):
    return 4 if rows % 64 == 0 else 2


def exchange_kernel(n_row, n_col, scale, block, partial, weight, out_grad,
                    activated, weight_grad, window_grad,
                    core_in, pair_out, pair_in, grads, grads_wide, cross_out, cross_in,
                    chain_out, chain_in, total, ready, local, local_out, piece_in, piece, step_in, whole,
                    core_sem, pair_sem, own_sem, far_sem, pass_sem, cross_sem,
                    chain_sem, piece_sem, step_sem, whole_sem):
    n_z, n_y = n_row // 2, n_col // 2
    row, col = lax.axis_index("row"), lax.axis_index("col")
    z, x = row // 2, row % 2
    y, core = col // 2, col % 2
    share = out_grad.shape[0]
    span = window_grad.shape[0]
    width = weight.shape[0]
    depth = width // n_col
    steps = n_row.bit_length() - 1
    cut = share // PARTS

    sibling = (row, y * 2 + 1 - core)
    mirror = (z * 2 + 1 - x, col)
    col_peers = [(row, (col + d) % n_col) for d in range(1, n_col)]
    swaps = []
    for s in range(steps):
        bit = 1 << s
        swaps.append((row + bit - row // bit % 2 * 2 * bit, col))
    ring = [((row + 2) % n_row, col), ((row + n_row - 2) % n_row, col)]

    barrier = pltpu.get_barrier_semaphore()
    greeted = col_peers + swaps + ring
    for device in greeted:
        pl.semaphore_signal(barrier, inc=1, device_id=device, device_id_type=MESH)
    pl.semaphore_wait(barrier, len(greeted))

    started = []

    def send(*args):
        copy = remote(*args)
        copy.start()
        started.append(copy)
        return copy

    def rows_of(index, length):
        if isinstance(index, int):
            return pl.ds(index * length, length)
        return pl.ds(pl.multiple_of(index * length, length), length)

    def part_of(owner, part):
        return rows_of(owner * PARTS + part, cut)

    core_copies = {}
    for d in list(range(1, n_y)) + [0]:
        for part in range(PARTS):
            owner = (y + d) % n_y * 2 + 1 - core
            core_copies[d, part] = send(
                partial.at[part_of(owner, part)], core_in.at[d, part],
                core_sem.at[0, d, part], core_sem.at[1, d, part], sibling)
    pair_copies = {}
    for part in range(PARTS):
        for d in range(1, n_y):
            core_copies[d, part].wait_recv()
            owner = (y + d) % n_y * 2 + core
            pair_out[d - 1, part] = (
                partial[part_of(owner, part), :].astype(F32) + core_in[d, part].astype(F32)
            ).astype(BF16)
            pair_copies[d, part] = send(
                pair_out.at[d - 1, part], pair_in.at[d - 1, part],
                pair_sem.at[0, d - 1, part], pair_sem.at[1, d - 1, part], (row, owner))

    far_copies, own_copies = {}, []
    for part in range(PARTS):
        core_copies[0, part].wait_recv()
        sums = partial[part_of(col, part), :].astype(F32) + core_in[0, part].astype(F32)
        for d in range(1, n_y):
            pair_copies[d, part].wait_recv()
            sums = sums + pair_in[d - 1, part].astype(F32)
        aggregated = sums.astype(BF16)
        pre_act = jnp.dot(aggregated, weight[...], preferred_element_type=F32)
        sigmoid_pre = jax.nn.sigmoid(pre_act)
        rows = pl.ds(part * cut, cut)
        grad_pre = (
            out_grad[rows, :].astype(F32) * sigmoid_pre * (1.0 + pre_act * (1.0 - sigmoid_pre))
        ).astype(BF16)
        grads[col, part] = lax.dot_general(
            weight[...], grad_pre, (((1,), (1,)), ((), ())), preferred_element_type=F32
        ).astype(BF16)
        mine = grads.at[col, part]
        for d in range(1, n_y):
            far_copies[d, part] = send(
                mine, mine, far_sem.at[0, d - 1, part], far_sem.at[1, d - 1, part],
                (row, (y + d) % n_y * 2 + core))
        own_copies.append(send(mine, mine, own_sem.at[0, part], own_sem.at[1, part], sibling))
        activated[rows, :] = (pre_act * sigmoid_pre).astype(BF16)
        outer = lax.dot_general(
            aggregated, grad_pre, (((0,), (0,)), ((), ())), preferred_element_type=F32
        )
        if part == 0:
            local[...] = outer
        else:
            local[...] += outer

    pass_copies = []
    for part in range(PARTS):
        for d in range(1, n_y):
            far_copies[d, part].wait_recv()
            got = grads.at[(y + n_y - d) % n_y * 2 + core, part]
            pass_copies.append(send(
                got, got, pass_sem.at[0, d - 1, part], pass_sem.at[1, d - 1, part], sibling))
    local_out[...] = local[...].astype(BF16)
    piece_copies = []
    for d in range(1, n_col):
        piece_copies.append(send(
            local_out.at[rows_of((col + d) % n_col, depth)], piece_in.at[d - 1],
            piece_sem.at[0, d - 1], piece_sem.at[1, d - 1], col_peers[d - 1]))
    for copy in own_copies + pass_copies:
        copy.wait_recv()
    for owner in range(n_col):
        for part in range(PARTS):
            grads_wide[:, part_of(owner, part)] = grads[owner, part]

    def columns_product(index, length):
        return jnp.dot(
            grads_wide[...], block[:, rows_of(index, length)], preferred_element_type=F32
        )

    narrow = span % LANES != 0
    if narrow:
        for tile in range(block.shape[1] // width):
            ready[rows_of(tile, width), :] = columns_product(tile, width).T

    def product(owner):
        if narrow:
            return ready[rows_of(owner, span), :]
        return columns_product(owner, span)

    high = (2 * z >= n_z).astype(jnp.int32)
    low_z = z + high * (n_z - 1 - 2 * z)

    def order(i):
        lead = n_z - 1 - 2 * low_z
        m = i - lead
        early = (m < 0).astype(jnp.int32)
        odd = jnp.abs(m) % 2
        late = (1 - odd) * (m // 2) + odd * (2 * low_z - m // 2)
        at = early * (n_z - 1 - i) + (1 - early) * late
        return at + high * (n_z - 1 - 2 * at)

    slabs = slabs_of(total.shape[0])
    slab = total.shape[0] // slabs

    def cross_copy(at, part):
        rows = pl.ds(part * slab, slab)
        return (cross_out.at[at, rows], cross_in.at[at, rows],
                cross_sem.at[0, at, part], cross_sem.at[1, at, part], mirror)

    swap_copies, whole_copies = [], []

    def next_swap(s):
        if s == 0:
            added = local[rows_of(col, depth), :]
            for copy in piece_copies:
                copy.wait_recv()
            for d in range(1, n_col):
                added = added + piece_in[d - 1].astype(F32)
        elif s <= steps:
            swap_copies[s - 1].wait_recv()
            added = piece[s - 1].astype(F32) + step_in[s - 1].astype(F32)
        if s < steps:
            piece[s] = added.astype(BF16)
            swap_copies.append(send(
                piece.at[s], step_in.at[s], step_sem.at[0, s], step_sem.at[1, s], swaps[s]))
        elif s == steps:
            spot = whole.at[rows_of(col, depth)]
            spot[...] = (added * scale).astype(BF16)
            for d in range(1, n_col):
                whole_copies.append(send(
                    spot, spot, whole_sem.at[0, d - 1], whole_sem.at[1, d - 1],
                    col_peers[d - 1]))

    def chain_copy(at, part):
        rows = pl.ds(part * slab, slab)
        up = (at > z).astype(jnp.int32)
        return remote(chain_out.at[at, rows], chain_in.at[up, at, rows],
                      chain_sem.at[0, up, at, part], chain_sem.at[1, up, at, part],
                      (row + 4 * up - 2, col))

    def await_chain(up, at, part):
        rows = pl.ds(part * slab, slab)
        remote(chain_out.at[at, rows], chain_in.at[up, at, rows],
               chain_sem.at[0, up, at, part], chain_sem.at[1, up, at, part], mirror).wait_recv()
        total[rows, :] += chain_in[up, at, rows, :].astype(F32)

    for i in range(n_z):
        at = order(i)
        cross_out[at] = product(at * 2 + 1 - x).astype(BF16)
        for part in range(slabs):
            send(*cross_copy(at, part))
        if i == 0:
            next_swap(0)
    for i in range(n_z):
        at = order(i)
        total[...] = product(at * 2 + x)
        for part in range(slabs):
            rows = pl.ds(part * slab, slab)
            remote(*cross_copy(at, part)).wait_recv()
            total[rows, :] += cross_in[at, rows, :].astype(F32)

            @pl.when(jnp.logical_and(z > 0, at >= z))
            def _():
                await_chain(1, at, part)

            @pl.when(jnp.logical_and(z < n_z - 1, at <= z))
            def _():
                await_chain(0, at, part)

            if i < n_z - 1:
                chain_out[at, rows, :] = total[rows, :].astype(BF16)
                chain_copy(at, part).start()
        if i == n_z - 1:
            result = total[...] if narrow else total[...].T
            window_grad[...] = result.astype(BF16)
        next_swap(i + 1)
    for s in range(n_z + 1, steps + 1):
        next_swap(s)
    for copy in whole_copies:
        copy.wait_recv()
    weight_grad[...] = whole[...].astype(F32)
    for copy in started:
        copy.wait_send()
    for i in range(n_z - 1):
        for part in range(slabs):
            chain_copy(order(i), part).wait_send()


def exchange(n_row, n_col, block, partial, weight, out_grad):
    rows, window = block.shape
    width = weight.shape[0]
    share = out_grad.shape[0]
    span = window // n_row
    n_z, n_y = n_row // 2, n_col // 2
    depth = width // n_col
    steps = n_row.bit_length() - 1
    cut = share // PARTS
    narrow = span % LANES != 0
    chunk = (span, width) if narrow else (width, span)
    slabs = slabs_of(chunk[0])
    dma = pltpu.SemaphoreType.DMA
    vmem = pl.BlockSpec(memory_space=pltpu.VMEM)
    return pl.pallas_call(
        functools.partial(exchange_kernel, n_row, n_col, 1.0 / math.sqrt(rows * n_row)),
        out_shape=(
            jax.ShapeDtypeStruct((share, width), BF16),
            jax.ShapeDtypeStruct((width, width), F32),
            jax.ShapeDtypeStruct((span, width), BF16),
        ),
        in_specs=[vmem, vmem, vmem, vmem],
        out_specs=(vmem, vmem, vmem),
        scratch_shapes=[
            pltpu.VMEM((n_y, PARTS, cut, width), BF16),
            pltpu.VMEM((n_y - 1, PARTS, cut, width), BF16),
            pltpu.VMEM((n_y - 1, PARTS, cut, width), BF16),
            pltpu.VMEM((n_col, PARTS, width, cut), BF16),
            pltpu.VMEM((width, rows), BF16),
            pltpu.VMEM((n_z, *chunk), BF16),
            pltpu.VMEM((n_z, *chunk), BF16),
            pltpu.VMEM((n_z, *chunk), BF16),
            pltpu.VMEM((2, n_z, *chunk), BF16),
            pltpu.VMEM(chunk, F32),
            pltpu.VMEM((window if narrow else 8, width), F32),
            pltpu.VMEM((width, width), F32),
            pltpu.VMEM((width, width), BF16),
            pltpu.VMEM((n_col - 1, depth, width), BF16),
            pltpu.VMEM((steps, depth, width), BF16),
            pltpu.VMEM((steps, depth, width), BF16),
            pltpu.VMEM((width, width), BF16),
            dma((2, n_y, PARTS)),
            dma((2, n_y - 1, PARTS)),
            dma((2, PARTS)),
            dma((2, n_y - 1, PARTS)),
            dma((2, n_y - 1, PARTS)),
            dma((2, n_z, slabs)),
            dma((2, 2, n_z, slabs)),
            dma((2, n_col - 1)),
            dma((2, steps)),
            dma((2, n_col - 1)),
        ],
        compiler_params=pltpu.CompilerParams(
            collective_id=0, has_side_effects=True, vmem_limit_bytes=40 * 1024 * 1024
        ),
    )(block, partial, weight, out_grad)


def on_device(n_row, n_col, tiles, tile_slot, tile_count, feats, weight, out_grad):
    held = [
        pltpu.with_memory_space_constraint(array, pltpu.HBM)
        for array in (tiles[0], tile_slot, feats)
    ]
    block, partial = block_product(held[0], held[1], tile_count, held[2])
    activated, weight_grad, window_grad = exchange(
        n_row, n_col, block, partial, weight, out_grad
    )
    activated, weight_grad, window_grad = publish(activated, weight_grad, window_grad)
    return activated, weight_grad, window_grad[None]


def solution(mesh):
    placed = (
        P("row", "col", None, None),
        P("row", "col"),
        P("row", "col"),
        P("col", None),
        P(),
        P(("row", "col"), None),
    )
    return jax.shard_map(
        functools.partial(on_device, mesh.shape["row"], mesh.shape["col"]),
        mesh=mesh,
        in_specs=placed,
        out_specs=(P(("row", "col"), None), P(), P("col", "row", None)),
        check_vma=False,
    )
```

```python
import functools
import math

import jax
import jax.numpy as jnp
from jax import lax
from jax.experimental import pallas as pl
from jax.experimental.pallas import tpu as pltpu
from jax.sharding import PartitionSpec as P

RT = 4
LANES = 128
PARTS = 2
MESH = pl.DeviceIdType.MESH
F32 = jnp.float32
BF16 = jnp.bfloat16


def block_kernel(slot_list, count, tiles, feats, block, partial, extra, source, total,
                 slots, first, others, following, list_sem, tile_sem, feat_sem):
    size = tiles.shape[1]
    col_tiles = feats.shape[0] // size
    places = RT * col_tiles

    list_copy = pltpu.make_async_copy(slot_list, slots, list_sem)
    list_copy.start()
    feat_copy = pltpu.make_async_copy(feats, source, feat_sem)
    feat_copy.start()

    def place_of(slot):
        row = pl.multiple_of(slot // col_tiles * size, size)
        column = pl.multiple_of(slot % col_tiles * size, size)
        return block.at[pl.ds(row, size), pl.ds(column, size)]

    for place in range(places):
        first[place] = -1
        others[place] = -1
    list_copy.wait()
    live = count[0, 0]

    @pl.loop(0, live)
    def _(position):
        slot = slots[0, position]
        taken = first[slot] >= 0

        @pl.when(jnp.logical_not(taken))
        def _():
            first[slot] = position
            pltpu.make_async_copy(tiles.at[position], place_of(slot), tile_sem.at[position]).start()

        @pl.when(taken)
        def _():
            following[position] = others[slot]
            others[slot] = position
            pltpu.make_async_copy(
                tiles.at[position], extra.at[position], tile_sem.at[position]
            ).start()

    @pl.loop(0, places)
    def _(place):
        @pl.when(first[place] < 0)
        def _():
            place_of(place)[...] = jnp.zeros((size, size), BF16)

    def await_tile(position):
        pltpu.make_async_copy(
            tiles.at[position], extra.at[position], tile_sem.at[position]
        ).wait()

    for row in range(RT):
        @pl.loop(row * col_tiles, (row + 1) * col_tiles)
        def _(place):
            @pl.when(first[place] >= 0)
            def _():
                await_tile(first[place])

                @pl.when(others[place] >= 0)
                def _():
                    spot = place_of(place)
                    total[...] = spot[...].astype(F32)

                    def add(position):
                        await_tile(position)
                        total[...] += extra[position].astype(F32)
                        return following[position]

                    lax.while_loop(lambda position: position >= 0, add, others[place])
                    spot[...] = total[...].astype(BF16)

        if row % 2 == 1:
            if row == 1:
                feat_copy.wait()
            rows = pl.ds((row - 1) * size, 2 * size)
            partial[rows, :] = jnp.dot(
                block[rows, :], source[...], preferred_element_type=F32
            ).astype(BF16)


def block_product(tiles, slots, count, feats):
    number, size, _ = tiles.shape
    window, width = feats.shape
    places = RT * window // size
    hbm = pl.BlockSpec(memory_space=pltpu.HBM)
    vmem = pl.BlockSpec(memory_space=pltpu.VMEM)
    return pl.pallas_call(
        block_kernel,
        out_shape=(
            jax.ShapeDtypeStruct((RT * size, window), BF16),
            jax.ShapeDtypeStruct((RT * size, width), BF16),
        ),
        in_specs=[hbm, pl.BlockSpec(memory_space=pltpu.SMEM), hbm, hbm],
        out_specs=(vmem, vmem),
        scratch_shapes=[
            pltpu.VMEM((number, size, size), BF16),
            pltpu.VMEM((window, width), BF16),
            pltpu.VMEM((size, size), F32),
            pltpu.SMEM(slots.shape, jnp.int32),
            pltpu.SMEM((places,), jnp.int32),
            pltpu.SMEM((places,), jnp.int32),
            pltpu.SMEM((number,), jnp.int32),
            pltpu.SemaphoreType.DMA,
            pltpu.SemaphoreType.DMA((number,)),
            pltpu.SemaphoreType.DMA,
        ],
        compiler_params=pltpu.CompilerParams(vmem_limit_bytes=24 * 1024 * 1024),
    )(slots, count, tiles, feats)


def publish_kernel(*refs):
    number = len(refs) // 2
    sem = refs[-1]
    copies = [
        pltpu.make_async_copy(refs[i], refs[number + i], sem.at[i]) for i in range(number)
    ]
    for copy in copies:
        copy.start()
    for copy in copies:
        copy.wait()


def publish(*results):
    held = [pltpu.with_memory_space_constraint(r, pltpu.VMEM) for r in results]
    return pl.pallas_call(
        publish_kernel,
        out_shape=tuple(jax.ShapeDtypeStruct(r.shape, r.dtype) for r in results),
        in_specs=[pl.BlockSpec(memory_space=pltpu.VMEM)] * len(results),
        out_specs=tuple(pl.BlockSpec(memory_space=pltpu.HBM) for _ in results),
        scratch_shapes=[pltpu.SemaphoreType.DMA((len(results),))],
    )(*held)


def remote(src, dst, send_sem, recv_sem, device):
    return pltpu.make_async_remote_copy(
        src_ref=src, dst_ref=dst, send_sem=send_sem, recv_sem=recv_sem,
        device_id=device, device_id_type=MESH,
    )


def exchange_kernel(n_row, n_col, scale, block, partial, weight, out_grad,
                    activated, weight_grad, window_grad,
                    core_in, straight_in, pair_out, pair_in, held_aggregated,
                    held_grad_pre, grads, grads_wide, cross_out, cross_in,
                    chain_out, chain_in, total, ready, local, local_out, piece_in, piece, step_in, whole,
                    core_sem, straight_sem, pair_sem, own_sem, far_sem, pass_sem, cross_sem,
                    chain_sem, piece_sem, step_sem, whole_sem):
    n_z, n_y = n_row // 2, n_col // 2
    row, col = lax.axis_index("row"), lax.axis_index("col")
    z, x = row // 2, row % 2
    y, core = col // 2, col % 2
    share = out_grad.shape[0]
    span = window_grad.shape[0]
    width = weight.shape[0]
    depth = width // n_col
    steps = n_row.bit_length() - 1
    cut = share // PARTS

    sibling = (row, y * 2 + 1 - core)
    mirror = (z * 2 + 1 - x, col)
    col_peers = [(row, (col + d) % n_col) for d in range(1, n_col)]
    swaps = []
    for s in range(steps):
        bit = 1 << s
        swaps.append((row + bit - row // bit % 2 * 2 * bit, col))
    ring = [((row + 2) % n_row, col), ((row + n_row - 2) % n_row, col)]

    barrier = pltpu.get_barrier_semaphore()
    greeted = col_peers + swaps + ring
    for device in greeted:
        pl.semaphore_signal(barrier, inc=1, device_id=device, device_id_type=MESH)
    pl.semaphore_wait(barrier, len(greeted))

    started = []

    def send(*args):
        copy = remote(*args)
        copy.start()
        started.append(copy)
        return copy

    def rows_of(index, length):
        if isinstance(index, int):
            return pl.ds(index * length, length)
        return pl.ds(pl.multiple_of(index * length, length), length)

    def part_of(owner, part):
        return rows_of(owner * PARTS + part, cut)

    core_copies = {}

    def to_sibling(d, part):
        owner = (y + d) % n_y * 2 + 1 - core
        core_copies[d, part] = send(
            partial.at[part_of(owner, part)], core_in.at[d, part],
            core_sem.at[0, d, part], core_sem.at[1, d, part], sibling)

    for part in range(1, PARTS):
        for d in range(1, n_y):
            to_sibling(d, part)
    for d in range(1, n_y):
        for k in range(2):
            owner = (y + d) % n_y * 2 + k
            send(partial.at[part_of(owner, 0)], straight_in.at[d - 1, core],
                 straight_sem.at[0, d - 1, k], straight_sem.at[1, d - 1, core], (row, owner))
    for part in range(PARTS):
        to_sibling(0, part)
    pair_copies = {}
    for part in range(1, PARTS):
        for d in range(1, n_y):
            core_copies[d, part].wait_recv()
            owner = (y + d) % n_y * 2 + core
            pair_out[d - 1, part] = (
                partial[part_of(owner, part), :].astype(F32) + core_in[d, part].astype(F32)
            ).astype(BF16)
            pair_copies[d, part] = send(
                pair_out.at[d - 1, part], pair_in.at[d - 1, part],
                pair_sem.at[0, d - 1, part], pair_sem.at[1, d - 1, part], (row, owner))

    own_copies = []
    for part in range(PARTS):
        last = part == PARTS - 1
        core_copies[0, part].wait_recv()
        sums = partial[part_of(col, part), :].astype(F32) + core_in[0, part].astype(F32)
        for d in range(1, n_y):
            if part == 0:
                for k in range(2):
                    remote(partial.at[part_of(0, 0)], straight_in.at[d - 1, k],
                           straight_sem.at[0, d - 1, k], straight_sem.at[1, d - 1, k],
                           sibling).wait_recv()
                    sums = sums + straight_in[d - 1, k].astype(F32)
            else:
                pair_copies[d, part].wait_recv()
                sums = sums + pair_in[d - 1, part].astype(F32)
        aggregated = sums.astype(BF16)
        pre_act = jnp.dot(aggregated, weight[...], preferred_element_type=F32)
        sigmoid_pre = jax.nn.sigmoid(pre_act)
        rows = pl.ds(part * cut, cut)
        grad_pre = (
            out_grad[rows, :].astype(F32) * sigmoid_pre * (1.0 + pre_act * (1.0 - sigmoid_pre))
        ).astype(BF16)
        grads[col, part] = lax.dot_general(
            weight[...], grad_pre, (((1,), (1,)), ((), ())), preferred_element_type=F32
        ).astype(BF16)
        mine = grads.at[col, part]
        for d in range(1, n_y):
            for turn in range(2 if last else 1):
                k = (core + turn) % 2
                send(mine, mine, far_sem.at[0, d - 1, part, turn],
                     far_sem.at[1, d - 1, part, turn], (row, (y + d) % n_y * 2 + k))
        own_copies.append(send(mine, mine, own_sem.at[0, part], own_sem.at[1, part], sibling))
        held_aggregated[rows, :] = aggregated
        held_grad_pre[rows, :] = grad_pre
        activated[rows, :] = (pre_act * sigmoid_pre).astype(BF16)

    local[...] = lax.dot_general(
        held_aggregated[...], held_grad_pre[...], (((0,), (0,)), ((), ())),
        preferred_element_type=F32,
    )

    def await_far(d, part, turn):
        got = grads.at[(y + n_y - d) % n_y * 2 + (core + turn) % 2, part]
        remote(got, got, far_sem.at[0, d - 1, part, turn], far_sem.at[1, d - 1, part, turn],
               sibling).wait_recv()
        return got

    pass_copies = []
    for part in range(PARTS - 1):
        for d in range(1, n_y):
            got = await_far(d, part, 0)
            pass_copies.append(send(
                got, got, pass_sem.at[0, d - 1, part], pass_sem.at[1, d - 1, part], sibling))
    for d in range(1, n_y):
        for turn in range(2):
            await_far(d, PARTS - 1, turn)
    local_out[...] = local[...].astype(BF16)
    piece_copies = []
    for d in range(1, n_col):
        piece_copies.append(send(
            local_out.at[rows_of((col + d) % n_col, depth)], piece_in.at[d - 1],
            piece_sem.at[0, d - 1], piece_sem.at[1, d - 1], col_peers[d - 1]))
    for copy in own_copies + pass_copies:
        copy.wait_recv()
    for owner in range(n_col):
        for part in range(PARTS):
            grads_wide[:, part_of(owner, part)] = grads[owner, part]

    def columns_product(index, length):
        return jnp.dot(
            grads_wide[...], block[:, rows_of(index, length)], preferred_element_type=F32
        )

    narrow = span % LANES != 0
    if narrow:
        for tile in range(block.shape[1] // width):
            ready[rows_of(tile, width), :] = columns_product(tile, width).T

    def product(owner):
        if narrow:
            return ready[rows_of(owner, span), :]
        return columns_product(owner, span)

    high = (2 * z >= n_z).astype(jnp.int32)
    low_z = z + high * (n_z - 1 - 2 * z)

    def order(i):
        lead = n_z - 1 - 2 * low_z
        m = i - lead
        early = (m < 0).astype(jnp.int32)
        odd = jnp.abs(m) % 2
        late = (1 - odd) * (m // 2) + odd * (2 * low_z - m // 2)
        at = early * (n_z - 1 - i) + (1 - early) * late
        return at + high * (n_z - 1 - 2 * at)

    slab = total.shape[0] // PARTS

    def cross_copy(at, part):
        rows = pl.ds(part * slab, slab)
        return (cross_out.at[at, rows], cross_in.at[at, rows],
                cross_sem.at[0, at, part], cross_sem.at[1, at, part], mirror)

    swap_copies, whole_copies = [], []

    def next_swap(s):
        if s == 0:
            added = local[rows_of(col, depth), :]
            for copy in piece_copies:
                copy.wait_recv()
            for d in range(1, n_col):
                added = added + piece_in[d - 1].astype(F32)
        elif s <= steps:
            swap_copies[s - 1].wait_recv()
            added = piece[s - 1].astype(F32) + step_in[s - 1].astype(F32)
        if s < steps:
            piece[s] = added.astype(BF16)
            swap_copies.append(send(
                piece.at[s], step_in.at[s], step_sem.at[0, s], step_sem.at[1, s], swaps[s]))
        elif s == steps:
            spot = whole.at[rows_of(col, depth)]
            spot[...] = (added * scale).astype(BF16)
            for d in range(1, n_col):
                whole_copies.append(send(
                    spot, spot, whole_sem.at[0, d - 1], whole_sem.at[1, d - 1],
                    col_peers[d - 1]))

    def chain_copy(at, part):
        rows = pl.ds(part * slab, slab)
        up = (at > z).astype(jnp.int32)
        return remote(chain_out.at[at, rows], chain_in.at[up, at, rows],
                      chain_sem.at[0, up, at, part], chain_sem.at[1, up, at, part],
                      (row + 4 * up - 2, col))

    def await_chain(up, at, part):
        rows = pl.ds(part * slab, slab)
        remote(chain_out.at[at, rows], chain_in.at[up, at, rows],
               chain_sem.at[0, up, at, part], chain_sem.at[1, up, at, part], mirror).wait_recv()
        total[rows, :] += chain_in[up, at, rows, :].astype(F32)

    for i in range(n_z):
        at = order(i)
        cross_out[at] = product(at * 2 + 1 - x).astype(BF16)
        for part in range(PARTS):
            send(*cross_copy(at, part))
        if i == 0:
            next_swap(0)
    for i in range(n_z):
        at = order(i)
        total[...] = product(at * 2 + x)
        for part in range(PARTS):
            rows = pl.ds(part * slab, slab)
            remote(*cross_copy(at, part)).wait_recv()
            total[rows, :] += cross_in[at, rows, :].astype(F32)

            @pl.when(jnp.logical_and(z > 0, at >= z))
            def _():
                await_chain(1, at, part)

            @pl.when(jnp.logical_and(z < n_z - 1, at <= z))
            def _():
                await_chain(0, at, part)

            if i < n_z - 1:
                chain_out[at, rows, :] = total[rows, :].astype(BF16)
                chain_copy(at, part).start()
        if i == n_z - 1:
            result = total[...] if narrow else total[...].T
            window_grad[...] = result.astype(BF16)
        next_swap(i + 1)
    for s in range(n_z + 1, steps + 1):
        next_swap(s)
    for copy in whole_copies:
        copy.wait_recv()
    weight_grad[...] = whole[...].astype(F32)
    for copy in started:
        copy.wait_send()
    for i in range(n_z - 1):
        for part in range(PARTS):
            chain_copy(order(i), part).wait_send()


def exchange(n_row, n_col, block, partial, weight, out_grad):
    rows, window = block.shape
    width = weight.shape[0]
    share = out_grad.shape[0]
    span = window // n_row
    n_z, n_y = n_row // 2, n_col // 2
    depth = width // n_col
    steps = n_row.bit_length() - 1
    cut = share // PARTS
    narrow = span % LANES != 0
    chunk = (span, width) if narrow else (width, span)
    dma = pltpu.SemaphoreType.DMA
    vmem = pl.BlockSpec(memory_space=pltpu.VMEM)
    return pl.pallas_call(
        functools.partial(exchange_kernel, n_row, n_col, 1.0 / math.sqrt(rows * n_row)),
        out_shape=(
            jax.ShapeDtypeStruct((share, width), BF16),
            jax.ShapeDtypeStruct((width, width), F32),
            jax.ShapeDtypeStruct((span, width), BF16),
        ),
        in_specs=[vmem, vmem, vmem, vmem],
        out_specs=(vmem, vmem, vmem),
        scratch_shapes=[
            pltpu.VMEM((n_y, PARTS, cut, width), BF16),
            pltpu.VMEM((n_y - 1, 2, cut, width), BF16),
            pltpu.VMEM((n_y - 1, PARTS, cut, width), BF16),
            pltpu.VMEM((n_y - 1, PARTS, cut, width), BF16),
            pltpu.VMEM((share, width), BF16),
            pltpu.VMEM((share, width), BF16),
            pltpu.VMEM((n_col, PARTS, width, cut), BF16),
            pltpu.VMEM((width, rows), BF16),
            pltpu.VMEM((n_z, *chunk), BF16),
            pltpu.VMEM((n_z, *chunk), BF16),
            pltpu.VMEM((n_z, *chunk), BF16),
            pltpu.VMEM((2, n_z, *chunk), BF16),
            pltpu.VMEM(chunk, F32),
            pltpu.VMEM((window if narrow else 8, width), F32),
            pltpu.VMEM((width, width), F32),
            pltpu.VMEM((width, width), BF16),
            pltpu.VMEM((n_col - 1, depth, width), BF16),
            pltpu.VMEM((steps, depth, width), BF16),
            pltpu.VMEM((steps, depth, width), BF16),
            pltpu.VMEM((width, width), BF16),
            dma((2, n_y, PARTS)),
            dma((2, n_y - 1, 2)),
            dma((2, n_y - 1, PARTS)),
            dma((2, PARTS)),
            dma((2, n_y - 1, PARTS, 2)),
            dma((2, n_y - 1, PARTS)),
            dma((2, n_z, PARTS)),
            dma((2, 2, n_z, PARTS)),
            dma((2, n_col - 1)),
            dma((2, steps)),
            dma((2, n_col - 1)),
        ],
        compiler_params=pltpu.CompilerParams(
            collective_id=0, has_side_effects=True, vmem_limit_bytes=40 * 1024 * 1024
        ),
    )(block, partial, weight, out_grad)


def on_device(n_row, n_col, tiles, tile_slot, tile_count, feats, weight, out_grad):
    held = [
        pltpu.with_memory_space_constraint(array, pltpu.HBM)
        for array in (tiles[0], tile_slot, feats)
    ]
    block, partial = block_product(held[0], held[1], tile_count, held[2])
    activated, weight_grad, window_grad = exchange(
        n_row, n_col, block, partial, weight, out_grad
    )
    activated, weight_grad, window_grad = publish(activated, weight_grad, window_grad)
    return activated, weight_grad, window_grad[None]


def solution(mesh):
    placed = (
        P("row", "col", None, None),
        P("row", "col"),
        P("row", "col"),
        P("col", None),
        P(),
        P(("row", "col"), None),
    )
    return jax.shard_map(
        functools.partial(on_device, mesh.shape["row"], mesh.shape["col"]),
        mesh=mesh,
        in_specs=placed,
        out_specs=(P(("row", "col"), None), P(), P("col", "row", None)),
        check_vma=False,
    )
```

```python
import functools
import math

import jax
import jax.numpy as jnp
from jax import lax
from jax.experimental import pallas as pl
from jax.experimental.pallas import tpu as pltpu
from jax.sharding import PartitionSpec as P

RT = 4
LANES = 128
PARTS = 2
MESH = pl.DeviceIdType.MESH
F32 = jnp.float32
BF16 = jnp.bfloat16


def block_kernel(slot_list, count, tiles, feats, block, partial, extra, source, total,
                 slots, first, others, following, list_sem, tile_sem, feat_sem):
    size = tiles.shape[1]
    col_tiles = feats.shape[0] // size
    places = RT * col_tiles

    list_copy = pltpu.make_async_copy(slot_list, slots, list_sem)
    list_copy.start()
    feat_copy = pltpu.make_async_copy(feats, source, feat_sem)
    feat_copy.start()

    def place_of(slot):
        row = pl.multiple_of(slot // col_tiles * size, size)
        column = pl.multiple_of(slot % col_tiles * size, size)
        return block.at[pl.ds(row, size), pl.ds(column, size)]

    for place in range(places):
        first[place] = -1
        others[place] = -1
    list_copy.wait()
    live = count[0, 0]

    @pl.loop(0, live)
    def _(position):
        slot = slots[0, position]
        taken = first[slot] >= 0

        @pl.when(jnp.logical_not(taken))
        def _():
            first[slot] = position
            pltpu.make_async_copy(tiles.at[position], place_of(slot), tile_sem.at[position]).start()

        @pl.when(taken)
        def _():
            following[position] = others[slot]
            others[slot] = position
            pltpu.make_async_copy(
                tiles.at[position], extra.at[position], tile_sem.at[position]
            ).start()

    @pl.loop(0, places)
    def _(place):
        @pl.when(first[place] < 0)
        def _():
            place_of(place)[...] = jnp.zeros((size, size), BF16)

    def await_tile(position):
        pltpu.make_async_copy(
            tiles.at[position], extra.at[position], tile_sem.at[position]
        ).wait()

    for row in range(RT):
        @pl.loop(row * col_tiles, (row + 1) * col_tiles)
        def _(place):
            @pl.when(first[place] >= 0)
            def _():
                await_tile(first[place])

                @pl.when(others[place] >= 0)
                def _():
                    spot = place_of(place)
                    total[...] = spot[...].astype(F32)

                    def add(position):
                        await_tile(position)
                        total[...] += extra[position].astype(F32)
                        return following[position]

                    lax.while_loop(lambda position: position >= 0, add, others[place])
                    spot[...] = total[...].astype(BF16)

        if row % 2 == 1:
            if row == 1:
                feat_copy.wait()
            rows = pl.ds((row - 1) * size, 2 * size)
            partial[rows, :] = jnp.dot(
                block[rows, :], source[...], preferred_element_type=F32
            ).astype(BF16)


def block_product(tiles, slots, count, feats):
    number, size, _ = tiles.shape
    window, width = feats.shape
    places = RT * window // size
    hbm = pl.BlockSpec(memory_space=pltpu.HBM)
    vmem = pl.BlockSpec(memory_space=pltpu.VMEM)
    return pl.pallas_call(
        block_kernel,
        out_shape=(
            jax.ShapeDtypeStruct((RT * size, window), BF16),
            jax.ShapeDtypeStruct((RT * size, width), BF16),
        ),
        in_specs=[hbm, pl.BlockSpec(memory_space=pltpu.SMEM), hbm, hbm],
        out_specs=(vmem, vmem),
        scratch_shapes=[
            pltpu.VMEM((number, size, size), BF16),
            pltpu.VMEM((window, width), BF16),
            pltpu.VMEM((size, size), F32),
            pltpu.SMEM(slots.shape, jnp.int32),
            pltpu.SMEM((places,), jnp.int32),
            pltpu.SMEM((places,), jnp.int32),
            pltpu.SMEM((number,), jnp.int32),
            pltpu.SemaphoreType.DMA,
            pltpu.SemaphoreType.DMA((number,)),
            pltpu.SemaphoreType.DMA,
        ],
        compiler_params=pltpu.CompilerParams(vmem_limit_bytes=24 * 1024 * 1024),
    )(slots, count, tiles, feats)


def publish_kernel(*refs):
    number = len(refs) // 2
    sem = refs[-1]
    copies = [
        pltpu.make_async_copy(refs[i], refs[number + i], sem.at[i]) for i in range(number)
    ]
    for copy in copies:
        copy.start()
    for copy in copies:
        copy.wait()


def publish(*results):
    held = [pltpu.with_memory_space_constraint(r, pltpu.VMEM) for r in results]
    return pl.pallas_call(
        publish_kernel,
        out_shape=tuple(jax.ShapeDtypeStruct(r.shape, r.dtype) for r in results),
        in_specs=[pl.BlockSpec(memory_space=pltpu.VMEM)] * len(results),
        out_specs=tuple(pl.BlockSpec(memory_space=pltpu.HBM) for _ in results),
        scratch_shapes=[pltpu.SemaphoreType.DMA((len(results),))],
    )(*held)


def remote(src, dst, send_sem, recv_sem, device):
    return pltpu.make_async_remote_copy(
        src_ref=src, dst_ref=dst, send_sem=send_sem, recv_sem=recv_sem,
        device_id=device, device_id_type=MESH,
    )


def slabs_of(rows):
    return 4 if rows % 64 == 0 else 2


def exchange_kernel(n_row, n_col, scale, block, partial, weight, out_grad,
                    activated, weight_grad, window_grad,
                    core_in, pair_out, pair_in, grads, grads_wide, cross_out, cross_in,
                    chain_out, chain_in, total, ready, held_aggregated, held_grad_pre,
                    local, half_out, half_in, piece_in, piece, step_in, whole,
                    core_sem, pair_sem, own_sem, far_sem, pass_sem, cross_sem,
                    chain_sem, half_sem, piece_sem, step_sem, whole_sem):
    n_z, n_y = n_row // 2, n_col // 2
    row, col = lax.axis_index("row"), lax.axis_index("col")
    z, x = row // 2, row % 2
    y, core = col // 2, col % 2
    share = out_grad.shape[0]
    span = window_grad.shape[0]
    width = weight.shape[0]
    depth = width // n_col
    steps = n_row.bit_length() - 2
    cut = share // PARTS

    sibling = (row, y * 2 + 1 - core)
    mirror = (z * 2 + 1 - x, col)
    col_peers = [(row, (col + d) % n_col) for d in range(1, n_col)]
    swaps = []
    for s in range(steps + 1):
        bit = 1 << s
        swaps.append((row + bit - row // bit % 2 * 2 * bit, col))
    ring = [((row + 2) % n_row, col), ((row + n_row - 2) % n_row, col)]

    barrier = pltpu.get_barrier_semaphore()
    greeted = col_peers + swaps + ring
    for device in greeted:
        pl.semaphore_signal(barrier, inc=1, device_id=device, device_id_type=MESH)
    pl.semaphore_wait(barrier, len(greeted))

    started = []

    def send(*args):
        copy = remote(*args)
        copy.start()
        started.append(copy)
        return copy

    def rows_of(index, length):
        if isinstance(index, int):
            return pl.ds(index * length, length)
        return pl.ds(pl.multiple_of(index * length, length), length)

    def part_of(owner, part):
        return rows_of(owner * PARTS + part, cut)

    core_copies = {}
    for d in list(range(1, n_y)) + [0]:
        for part in range(PARTS):
            owner = (y + d) % n_y * 2 + 1 - core
            core_copies[d, part] = send(
                partial.at[part_of(owner, part)], core_in.at[d, part],
                core_sem.at[0, d, part], core_sem.at[1, d, part], sibling)
    pair_copies = {}
    for part in range(PARTS):
        for d in range(1, n_y):
            core_copies[d, part].wait_recv()
            owner = (y + d) % n_y * 2 + core
            pair_out[d - 1, part] = (
                partial[part_of(owner, part), :].astype(F32) + core_in[d, part].astype(F32)
            ).astype(BF16)
            pair_copies[d, part] = send(
                pair_out.at[d - 1, part], pair_in.at[d - 1, part],
                pair_sem.at[0, d - 1, part], pair_sem.at[1, d - 1, part], (row, owner))

    far_copies, own_copies = {}, []
    for part in range(PARTS):
        core_copies[0, part].wait_recv()
        sums = partial[part_of(col, part), :].astype(F32) + core_in[0, part].astype(F32)
        for d in range(1, n_y):
            pair_copies[d, part].wait_recv()
            sums = sums + pair_in[d - 1, part].astype(F32)
        aggregated = sums.astype(BF16)
        pre_act = jnp.dot(aggregated, weight[...], preferred_element_type=F32)
        sigmoid_pre = jax.nn.sigmoid(pre_act)
        rows = pl.ds(part * cut, cut)
        grad_pre = (
            out_grad[rows, :].astype(F32) * sigmoid_pre * (1.0 + pre_act * (1.0 - sigmoid_pre))
        ).astype(BF16)
        grads[col, part] = lax.dot_general(
            weight[...], grad_pre, (((1,), (1,)), ((), ())), preferred_element_type=F32
        ).astype(BF16)
        mine = grads.at[col, part]
        for d in range(1, n_y):
            far_copies[d, part] = send(
                mine, mine, far_sem.at[0, d - 1, part], far_sem.at[1, d - 1, part],
                (row, (y + d) % n_y * 2 + core))
        own_copies.append(send(mine, mine, own_sem.at[0, part], own_sem.at[1, part], sibling))
        held_aggregated[rows, :] = aggregated
        held_grad_pre[rows, :] = grad_pre
        activated[rows, :] = (pre_act * sigmoid_pre).astype(BF16)

    half = width // 2
    local[...] = lax.dot_general(
        held_aggregated[...], held_grad_pre[...], (((0,), (0,)), ((), ())),
        preferred_element_type=F32,
    )
    half_out[0] = local[rows_of(1 - core, half), :].astype(BF16)
    half_copy = send(half_out.at[0], half_in.at[0], half_sem.at[0, 0], half_sem.at[1, 0], sibling)

    pass_copies = []
    for part in range(PARTS):
        for d in range(1, n_y):
            far_copies[d, part].wait_recv()
            got = grads.at[(y + n_y - d) % n_y * 2 + core, part]
            pass_copies.append(send(
                got, got, pass_sem.at[0, d - 1, part], pass_sem.at[1, d - 1, part], sibling))
    half_copy.wait_recv()
    half_out[1] = (local[rows_of(core, half), :] + half_in[0].astype(F32)).astype(BF16)
    half_copy = send(half_out.at[1], half_in.at[1], half_sem.at[0, 1], half_sem.at[1, 1], mirror)
    for copy in own_copies + pass_copies:
        copy.wait_recv()
    for owner in range(n_col):
        for part in range(PARTS):
            grads_wide[:, part_of(owner, part)] = grads[owner, part]

    def columns_product(index, length):
        return jnp.dot(
            grads_wide[...], block[:, rows_of(index, length)], preferred_element_type=F32
        )

    narrow = span % LANES != 0
    if narrow:
        for tile in range(block.shape[1] // width):
            ready[rows_of(tile, width), :] = columns_product(tile, width).T

    def product(owner):
        if narrow:
            return ready[rows_of(owner, span), :]
        return columns_product(owner, span)

    high = (2 * z >= n_z).astype(jnp.int32)
    low_z = z + high * (n_z - 1 - 2 * z)

    def order(i):
        lead = n_z - 1 - 2 * low_z
        m = i - lead
        early = (m < 0).astype(jnp.int32)
        odd = jnp.abs(m) % 2
        late = (1 - odd) * (m // 2) + odd * (2 * low_z - m // 2)
        at = early * (n_z - 1 - i) + (1 - early) * late
        return at + high * (n_z - 1 - 2 * at)

    slabs = slabs_of(total.shape[0])
    slab = total.shape[0] // slabs

    def cross_copy(at, part):
        rows = pl.ds(part * slab, slab)
        return (cross_out.at[at, rows], cross_in.at[at, rows],
                cross_sem.at[0, at, part], cross_sem.at[1, at, part], mirror)

    piece_copies, swap_copies, whole_copies = [], [], []
    place = core * n_y + y

    def cut_along_y():
        half_copy.wait_recv()
        local[pl.ds(0, half), :] = half_out[1].astype(F32) + half_in[1].astype(F32)
        half_out[2] = local[pl.ds(0, half), :].astype(BF16)
        for d in range(1, n_y):
            at = (y + d) % n_y
            piece_copies.append(send(
                half_out.at[2, rows_of(at, depth)], piece_in.at[d - 1],
                piece_sem.at[0, d - 1], piece_sem.at[1, d - 1], (row, at * 2 + core)))

    def next_swap(s):
        if s == 0:
            added = local[rows_of(y, depth), :]
            for copy in piece_copies:
                copy.wait_recv()
            for d in range(1, n_y):
                added = added + piece_in[d - 1].astype(F32)
        elif s <= steps:
            swap_copies[s - 1].wait_recv()
            added = piece[s - 1].astype(F32) + step_in[s - 1].astype(F32)
        if s < steps:
            piece[s] = added.astype(BF16)
            swap_copies.append(send(
                piece.at[s], step_in.at[s], step_sem.at[0, s], step_sem.at[1, s], swaps[s + 1]))
        elif s == steps:
            spot = whole.at[rows_of(place, depth)]
            spot[...] = (added * scale).astype(BF16)
            for d in range(1, n_col):
                whole_copies.append(send(
                    spot, spot, whole_sem.at[0, d - 1], whole_sem.at[1, d - 1],
                    col_peers[d - 1]))

    def chain_copy(at, part):
        rows = pl.ds(part * slab, slab)
        up = (at > z).astype(jnp.int32)
        return remote(chain_out.at[at, rows], chain_in.at[up, at, rows],
                      chain_sem.at[0, up, at, part], chain_sem.at[1, up, at, part],
                      (row + 4 * up - 2, col))

    def await_chain(up, at, part):
        rows = pl.ds(part * slab, slab)
        remote(chain_out.at[at, rows], chain_in.at[up, at, rows],
               chain_sem.at[0, up, at, part], chain_sem.at[1, up, at, part], mirror).wait_recv()
        total[rows, :] += chain_in[up, at, rows, :].astype(F32)

    for i in range(n_z):
        at = order(i)
        cross_out[at] = product(at * 2 + 1 - x).astype(BF16)
        for part in range(slabs):
            send(*cross_copy(at, part))
        if i == min(1, n_z - 1):
            cut_along_y()
    for i in range(n_z):
        at = order(i)
        total[...] = product(at * 2 + x)
        for part in range(slabs):
            rows = pl.ds(part * slab, slab)
            remote(*cross_copy(at, part)).wait_recv()
            total[rows, :] += cross_in[at, rows, :].astype(F32)

            @pl.when(jnp.logical_and(z > 0, at >= z))
            def _():
                await_chain(1, at, part)

            @pl.when(jnp.logical_and(z < n_z - 1, at <= z))
            def _():
                await_chain(0, at, part)

            if i < n_z - 1:
                chain_out[at, rows, :] = total[rows, :].astype(BF16)
                chain_copy(at, part).start()
        if i == n_z - 1:
            result = total[...] if narrow else total[...].T
            window_grad[...] = result.astype(BF16)
        next_swap(i)
    for s in range(n_z, steps + 1):
        next_swap(s)
    for copy in whole_copies:
        copy.wait_recv()
    weight_grad[...] = whole[...].astype(F32)
    for copy in started:
        copy.wait_send()
    for i in range(n_z - 1):
        for part in range(slabs):
            chain_copy(order(i), part).wait_send()


def exchange(n_row, n_col, block, partial, weight, out_grad):
    rows, window = block.shape
    width = weight.shape[0]
    share = out_grad.shape[0]
    span = window // n_row
    n_z, n_y = n_row // 2, n_col // 2
    depth = width // n_col
    steps = n_row.bit_length() - 2
    cut = share // PARTS
    narrow = span % LANES != 0
    chunk = (span, width) if narrow else (width, span)
    slabs = slabs_of(chunk[0])
    dma = pltpu.SemaphoreType.DMA
    vmem = pl.BlockSpec(memory_space=pltpu.VMEM)
    return pl.pallas_call(
        functools.partial(exchange_kernel, n_row, n_col, 1.0 / math.sqrt(rows * n_row)),
        out_shape=(
            jax.ShapeDtypeStruct((share, width), BF16),
            jax.ShapeDtypeStruct((width, width), F32),
            jax.ShapeDtypeStruct((span, width), BF16),
        ),
        in_specs=[vmem, vmem, vmem, vmem],
        out_specs=(vmem, vmem, vmem),
        scratch_shapes=[
            pltpu.VMEM((n_y, PARTS, cut, width), BF16),
            pltpu.VMEM((n_y - 1, PARTS, cut, width), BF16),
            pltpu.VMEM((n_y - 1, PARTS, cut, width), BF16),
            pltpu.VMEM((n_col, PARTS, width, cut), BF16),
            pltpu.VMEM((width, rows), BF16),
            pltpu.VMEM((n_z, *chunk), BF16),
            pltpu.VMEM((n_z, *chunk), BF16),
            pltpu.VMEM((n_z, *chunk), BF16),
            pltpu.VMEM((2, n_z, *chunk), BF16),
            pltpu.VMEM(chunk, F32),
            pltpu.VMEM((window if narrow else 8, width), F32),
            pltpu.VMEM((share, width), BF16),
            pltpu.VMEM((share, width), BF16),
            pltpu.VMEM((width, width), F32),
            pltpu.VMEM((3, width // 2, width), BF16),
            pltpu.VMEM((2, width // 2, width), BF16),
            pltpu.VMEM((n_y - 1, depth, width), BF16),
            pltpu.VMEM((steps, depth, width), BF16),
            pltpu.VMEM((steps, depth, width), BF16),
            pltpu.VMEM((width, width), BF16),
            dma((2, n_y, PARTS)),
            dma((2, n_y - 1, PARTS)),
            dma((2, PARTS)),
            dma((2, n_y - 1, PARTS)),
            dma((2, n_y - 1, PARTS)),
            dma((2, n_z, slabs)),
            dma((2, 2, n_z, slabs)),
            dma((2, 2)),
            dma((2, n_y - 1)),
            dma((2, steps)),
            dma((2, n_col - 1)),
        ],
        compiler_params=pltpu.CompilerParams(
            collective_id=0, has_side_effects=True, vmem_limit_bytes=40 * 1024 * 1024
        ),
    )(block, partial, weight, out_grad)


def on_device(n_row, n_col, tiles, tile_slot, tile_count, feats, weight, out_grad):
    held = [
        pltpu.with_memory_space_constraint(array, pltpu.HBM)
        for array in (tiles[0], tile_slot, feats)
    ]
    block, partial = block_product(held[0], held[1], tile_count, held[2])
    activated, weight_grad, window_grad = exchange(
        n_row, n_col, block, partial, weight, out_grad
    )
    activated, weight_grad, window_grad = publish(activated, weight_grad, window_grad)
    return activated, weight_grad, window_grad[None]


def solution(mesh):
    placed = (
        P("row", "col", None, None),
        P("row", "col"),
        P("row", "col"),
        P("col", None),
        P(),
        P(("row", "col"), None),
    )
    return jax.shard_map(
        functools.partial(on_device, mesh.shape["row"], mesh.shape["col"]),
        mesh=mesh,
        in_specs=placed,
        out_specs=(P(("row", "col"), None), P(), P("col", "row", None)),
        check_vma=False,
    )
```

```python
import functools
import math

import jax
import jax.numpy as jnp
from jax import lax
from jax.experimental import pallas as pl
from jax.experimental.pallas import tpu as pltpu
from jax.sharding import PartitionSpec as P

RT = 4
LANES = 128
PARTS = 2
MESH = pl.DeviceIdType.MESH
F32 = jnp.float32
BF16 = jnp.bfloat16


def block_kernel(slot_list, count, tiles, feats, block, partial, extra, source, total,
                 slots, first, others, following, list_sem, tile_sem, feat_sem):
    size = tiles.shape[1]
    col_tiles = feats.shape[0] // size
    places = RT * col_tiles

    list_copy = pltpu.make_async_copy(slot_list, slots, list_sem)
    list_copy.start()
    feat_copy = pltpu.make_async_copy(feats, source, feat_sem)
    feat_copy.start()

    def place_of(slot):
        row = pl.multiple_of(slot // col_tiles * size, size)
        column = pl.multiple_of(slot % col_tiles * size, size)
        return block.at[pl.ds(row, size), pl.ds(column, size)]

    for place in range(places):
        first[place] = -1
        others[place] = -1
    block[...] = jnp.zeros_like(block)
    list_copy.wait()
    live = count[0, 0]

    @pl.loop(0, live)
    def _(position):
        slot = slots[0, position]
        taken = first[slot] >= 0

        @pl.when(jnp.logical_not(taken))
        def _():
            first[slot] = position
            pltpu.make_async_copy(tiles.at[position], place_of(slot), tile_sem.at[position]).start()

        @pl.when(taken)
        def _():
            following[position] = others[slot]
            others[slot] = position
            pltpu.make_async_copy(
                tiles.at[position], extra.at[position], tile_sem.at[position]
            ).start()

    def await_tile(position):
        pltpu.make_async_copy(
            tiles.at[position], extra.at[position], tile_sem.at[position]
        ).wait()

    for row in range(RT):
        @pl.loop(row * col_tiles, (row + 1) * col_tiles)
        def _(place):
            @pl.when(first[place] >= 0)
            def _():
                await_tile(first[place])

                @pl.when(others[place] >= 0)
                def _():
                    spot = place_of(place)
                    total[...] = spot[...].astype(F32)

                    def add(position):
                        await_tile(position)
                        total[...] += extra[position].astype(F32)
                        return following[position]

                    lax.while_loop(lambda position: position >= 0, add, others[place])
                    spot[...] = total[...].astype(BF16)

        if row % 2 == 1:
            if row == 1:
                feat_copy.wait()
            rows = pl.ds((row - 1) * size, 2 * size)
            partial[rows, :] = jnp.dot(
                block[rows, :], source[...], preferred_element_type=F32
            ).astype(BF16)


def block_product(tiles, slots, count, feats):
    number, size, _ = tiles.shape
    window, width = feats.shape
    places = RT * window // size
    hbm = pl.BlockSpec(memory_space=pltpu.HBM)
    vmem = pl.BlockSpec(memory_space=pltpu.VMEM)
    return pl.pallas_call(
        block_kernel,
        out_shape=(
            jax.ShapeDtypeStruct((RT * size, window), BF16),
            jax.ShapeDtypeStruct((RT * size, width), BF16),
        ),
        in_specs=[hbm, pl.BlockSpec(memory_space=pltpu.SMEM), hbm, hbm],
        out_specs=(vmem, vmem),
        scratch_shapes=[
            pltpu.VMEM((number, size, size), BF16),
            pltpu.VMEM((window, width), BF16),
            pltpu.VMEM((size, size), F32),
            pltpu.SMEM(slots.shape, jnp.int32),
            pltpu.SMEM((places,), jnp.int32),
            pltpu.SMEM((places,), jnp.int32),
            pltpu.SMEM((number,), jnp.int32),
            pltpu.SemaphoreType.DMA,
            pltpu.SemaphoreType.DMA((number,)),
            pltpu.SemaphoreType.DMA,
        ],
        compiler_params=pltpu.CompilerParams(vmem_limit_bytes=24 * 1024 * 1024),
    )(slots, count, tiles, feats)


def publish_kernel(*refs):
    number = len(refs) // 2
    sem = refs[-1]
    copies = [
        pltpu.make_async_copy(refs[i], refs[number + i], sem.at[i]) for i in range(number)
    ]
    for copy in copies:
        copy.start()
    for copy in copies:
        copy.wait()


def publish(*results):
    held = [pltpu.with_memory_space_constraint(r, pltpu.VMEM) for r in results]
    return pl.pallas_call(
        publish_kernel,
        out_shape=tuple(jax.ShapeDtypeStruct(r.shape, r.dtype) for r in results),
        in_specs=[pl.BlockSpec(memory_space=pltpu.VMEM)] * len(results),
        out_specs=tuple(pl.BlockSpec(memory_space=pltpu.HBM) for _ in results),
        scratch_shapes=[pltpu.SemaphoreType.DMA((len(results),))],
    )(*held)


def remote(src, dst, send_sem, recv_sem, device):
    return pltpu.make_async_remote_copy(
        src_ref=src, dst_ref=dst, send_sem=send_sem, recv_sem=recv_sem,
        device_id=device, device_id_type=MESH,
    )


def slabs_of(rows):
    return 4 if rows % 64 == 0 else 2


def exchange_kernel(n_row, n_col, scale, block, partial, weight, out_grad,
                    activated, weight_grad, window_grad,
                    core_in, pair_out, pair_in, grads, grads_wide, cross_out, cross_in,
                    chain_out, chain_in, total, ready, held_aggregated, held_grad_pre,
                    local, half_out, half_in, piece_in, piece, step_in, whole,
                    core_sem, pair_sem, own_sem, far_sem, pass_sem, cross_sem,
                    chain_sem, half_sem, piece_sem, step_sem, whole_sem):
    n_z, n_y = n_row // 2, n_col // 2
    row, col = lax.axis_index("row"), lax.axis_index("col")
    z, x = row // 2, row % 2
    y, core = col // 2, col % 2
    share = out_grad.shape[0]
    span = window_grad.shape[0]
    width = weight.shape[0]
    depth = width // n_col
    steps = n_row.bit_length() - 2
    cut = share // PARTS

    sibling = (row, y * 2 + 1 - core)
    mirror = (z * 2 + 1 - x, col)
    col_peers = [(row, (col + d) % n_col) for d in range(1, n_col)]
    swaps = []
    for s in range(steps + 1):
        bit = 1 << s
        swaps.append((row + bit - row // bit % 2 * 2 * bit, col))
    ring = [((row + 2) % n_row, col), ((row + n_row - 2) % n_row, col)]

    barrier = pltpu.get_barrier_semaphore()
    greeted = col_peers + swaps + ring
    for device in greeted:
        pl.semaphore_signal(barrier, inc=1, device_id=device, device_id_type=MESH)
    pl.semaphore_wait(barrier, len(greeted))

    started = []

    def send(*args):
        copy = remote(*args)
        copy.start()
        started.append(copy)
        return copy

    def rows_of(index, length):
        if isinstance(index, int):
            return pl.ds(index * length, length)
        return pl.ds(pl.multiple_of(index * length, length), length)

    def part_of(owner, part):
        return rows_of(owner * PARTS + part, cut)

    core_copies = {}
    for d in list(range(1, n_y)) + [0]:
        for part in range(PARTS):
            owner = (y + d) % n_y * 2 + 1 - core
            core_copies[d, part] = send(
                partial.at[part_of(owner, part)], core_in.at[d, part],
                core_sem.at[0, d, part], core_sem.at[1, d, part], sibling)
    pair_copies = {}
    for part in range(PARTS):
        for d in range(1, n_y):
            core_copies[d, part].wait_recv()
            owner = (y + d) % n_y * 2 + core
            pair_out[d - 1, part] = (
                partial[part_of(owner, part), :].astype(F32) + core_in[d, part].astype(F32)
            ).astype(BF16)
            pair_copies[d, part] = send(
                pair_out.at[d - 1, part], pair_in.at[d - 1, part],
                pair_sem.at[0, d - 1, part], pair_sem.at[1, d - 1, part], (row, owner))

    far_copies, own_copies = {}, []
    for part in range(PARTS):
        core_copies[0, part].wait_recv()
        sums = partial[part_of(col, part), :].astype(F32) + core_in[0, part].astype(F32)
        for d in range(1, n_y):
            pair_copies[d, part].wait_recv()
            sums = sums + pair_in[d - 1, part].astype(F32)
        aggregated = sums.astype(BF16)
        pre_act = jnp.dot(aggregated, weight[...], preferred_element_type=F32)
        sigmoid_pre = jax.nn.sigmoid(pre_act)
        rows = pl.ds(part * cut, cut)
        grad_pre = (
            out_grad[rows, :].astype(F32) * sigmoid_pre * (1.0 + pre_act * (1.0 - sigmoid_pre))
        ).astype(BF16)
        grads[col, part] = lax.dot_general(
            weight[...], grad_pre, (((1,), (1,)), ((), ())), preferred_element_type=F32
        ).astype(BF16)
        mine = grads.at[col, part]
        for d in range(1, n_y):
            far_copies[d, part] = send(
                mine, mine, far_sem.at[0, d - 1, part], far_sem.at[1, d - 1, part],
                (row, (y + d) % n_y * 2 + core))
        own_copies.append(send(mine, mine, own_sem.at[0, part], own_sem.at[1, part], sibling))
        held_aggregated[rows, :] = aggregated
        held_grad_pre[rows, :] = grad_pre
        activated[rows, :] = (pre_act * sigmoid_pre).astype(BF16)

    half = width // 2
    local[...] = lax.dot_general(
        held_aggregated[...], held_grad_pre[...], (((0,), (0,)), ((), ())),
        preferred_element_type=F32,
    )
    half_out[0] = local[rows_of(1 - core, half), :].astype(BF16)
    half_copy = send(half_out.at[0], half_in.at[0], half_sem.at[0, 0], half_sem.at[1, 0], sibling)

    pass_copies = []
    for part in range(PARTS):
        for d in range(1, n_y):
            far_copies[d, part].wait_recv()
            got = grads.at[(y + n_y - d) % n_y * 2 + core, part]
            pass_copies.append(send(
                got, got, pass_sem.at[0, d - 1, part], pass_sem.at[1, d - 1, part], sibling))
    half_copy.wait_recv()
    half_out[1] = (local[rows_of(core, half), :] + half_in[0].astype(F32)).astype(BF16)
    half_copy = send(half_out.at[1], half_in.at[1], half_sem.at[0, 1], half_sem.at[1, 1], mirror)
    for copy in own_copies + pass_copies:
        copy.wait_recv()
    for owner in range(n_col):
        for part in range(PARTS):
            grads_wide[:, part_of(owner, part)] = grads[owner, part]

    def columns_product(index, length):
        return jnp.dot(
            grads_wide[...], block[:, rows_of(index, length)], preferred_element_type=F32
        )

    narrow = span % LANES != 0
    if narrow:
        for tile in range(block.shape[1] // width):
            ready[rows_of(tile, width), :] = columns_product(tile, width).T

    def product(owner):
        if narrow:
            return ready[rows_of(owner, span), :]
        return columns_product(owner, span)

    high = (2 * z >= n_z).astype(jnp.int32)
    low_z = z + high * (n_z - 1 - 2 * z)

    def order(i):
        lead = n_z - 1 - 2 * low_z
        m = i - lead
        early = (m < 0).astype(jnp.int32)
        odd = jnp.abs(m) % 2
        late = (1 - odd) * (m // 2) + odd * (2 * low_z - m // 2)
        at = early * (n_z - 1 - i) + (1 - early) * late
        return at + high * (n_z - 1 - 2 * at)

    slabs = slabs_of(total.shape[0])
    slab = total.shape[0] // slabs

    def cross_copy(at, part):
        rows = pl.ds(part * slab, slab)
        return (cross_out.at[at, rows], cross_in.at[at, rows],
                cross_sem.at[0, at, part], cross_sem.at[1, at, part], mirror)

    piece_copies, swap_copies, whole_copies = [], [], []
    place = core * n_y + y

    def cut_along_y():
        half_copy.wait_recv()
        local[pl.ds(0, half), :] = half_out[1].astype(F32) + half_in[1].astype(F32)
        half_out[2] = local[pl.ds(0, half), :].astype(BF16)
        for d in range(1, n_y):
            at = (y + d) % n_y
            piece_copies.append(send(
                half_out.at[2, rows_of(at, depth)], piece_in.at[d - 1],
                piece_sem.at[0, d - 1], piece_sem.at[1, d - 1], (row, at * 2 + core)))

    def next_swap(s):
        if s == 0:
            added = local[rows_of(y, depth), :]
            for copy in piece_copies:
                copy.wait_recv()
            for d in range(1, n_y):
                added = added + piece_in[d - 1].astype(F32)
        elif s <= steps:
            swap_copies[s - 1].wait_recv()
            added = piece[s - 1].astype(F32) + step_in[s - 1].astype(F32)
        if s < steps:
            piece[s] = added.astype(BF16)
            swap_copies.append(send(
                piece.at[s], step_in.at[s], step_sem.at[0, s], step_sem.at[1, s], swaps[s + 1]))
        elif s == steps:
            spot = whole.at[rows_of(place, depth)]
            spot[...] = (added * scale).astype(BF16)
            for d in range(1, n_col):
                whole_copies.append(send(
                    spot, spot, whole_sem.at[0, d - 1], whole_sem.at[1, d - 1],
                    col_peers[d - 1]))

    def chain_copy(at, part):
        rows = pl.ds(part * slab, slab)
        up = (at > z).astype(jnp.int32)
        return remote(chain_out.at[at, rows], chain_in.at[up, at, rows],
                      chain_sem.at[0, up, at, part], chain_sem.at[1, up, at, part],
                      (row + 4 * up - 2, col))

    def await_chain(up, at, part):
        rows = pl.ds(part * slab, slab)
        remote(chain_out.at[at, rows], chain_in.at[up, at, rows],
               chain_sem.at[0, up, at, part], chain_sem.at[1, up, at, part], mirror).wait_recv()
        total[rows, :] += chain_in[up, at, rows, :].astype(F32)

    for i in range(n_z):
        at = order(i)
        cross_out[at] = product(at * 2 + 1 - x).astype(BF16)
        for part in range(slabs):
            send(*cross_copy(at, part))
        if i == min(1, n_z - 1):
            cut_along_y()
    for i in range(n_z):
        at = order(i)
        total[...] = product(at * 2 + x)
        for part in range(slabs):
            rows = pl.ds(part * slab, slab)
            remote(*cross_copy(at, part)).wait_recv()
            total[rows, :] += cross_in[at, rows, :].astype(F32)

            @pl.when(jnp.logical_and(z > 0, at >= z))
            def _():
                await_chain(1, at, part)

            @pl.when(jnp.logical_and(z < n_z - 1, at <= z))
            def _():
                await_chain(0, at, part)

            if i < n_z - 1:
                chain_out[at, rows, :] = total[rows, :].astype(BF16)
                chain_copy(at, part).start()
        if i == n_z - 1:
            result = total[...] if narrow else total[...].T
            window_grad[...] = result.astype(BF16)
        next_swap(i)
    for s in range(n_z, steps + 1):
        next_swap(s)
    for copy in whole_copies:
        copy.wait_recv()
    weight_grad[...] = whole[...].astype(F32)
    for copy in started:
        copy.wait_send()
    for i in range(n_z - 1):
        for part in range(slabs):
            chain_copy(order(i), part).wait_send()


def exchange(n_row, n_col, block, partial, weight, out_grad):
    rows, window = block.shape
    width = weight.shape[0]
    share = out_grad.shape[0]
    span = window // n_row
    n_z, n_y = n_row // 2, n_col // 2
    depth = width // n_col
    steps = n_row.bit_length() - 2
    cut = share // PARTS
    narrow = span % LANES != 0
    chunk = (span, width) if narrow else (width, span)
    slabs = slabs_of(chunk[0])
    dma = pltpu.SemaphoreType.DMA
    vmem = pl.BlockSpec(memory_space=pltpu.VMEM)
    return pl.pallas_call(
        functools.partial(exchange_kernel, n_row, n_col, 1.0 / math.sqrt(rows * n_row)),
        out_shape=(
            jax.ShapeDtypeStruct((share, width), BF16),
            jax.ShapeDtypeStruct((width, width), F32),
            jax.ShapeDtypeStruct((span, width), BF16),
        ),
        in_specs=[vmem, vmem, vmem, vmem],
        out_specs=(vmem, vmem, vmem),
        scratch_shapes=[
            pltpu.VMEM((n_y, PARTS, cut, width), BF16),
            pltpu.VMEM((n_y - 1, PARTS, cut, width), BF16),
            pltpu.VMEM((n_y - 1, PARTS, cut, width), BF16),
            pltpu.VMEM((n_col, PARTS, width, cut), BF16),
            pltpu.VMEM((width, rows), BF16),
            pltpu.VMEM((n_z, *chunk), BF16),
            pltpu.VMEM((n_z, *chunk), BF16),
            pltpu.VMEM((n_z, *chunk), BF16),
            pltpu.VMEM((2, n_z, *chunk), BF16),
            pltpu.VMEM(chunk, F32),
            pltpu.VMEM((window if narrow else 8, width), F32),
            pltpu.VMEM((share, width), BF16),
            pltpu.VMEM((share, width), BF16),
            pltpu.VMEM((width, width), F32),
            pltpu.VMEM((3, width // 2, width), BF16),
            pltpu.VMEM((2, width // 2, width), BF16),
            pltpu.VMEM((n_y - 1, depth, width), BF16),
            pltpu.VMEM((steps, depth, width), BF16),
            pltpu.VMEM((steps, depth, width), BF16),
            pltpu.VMEM((width, width), BF16),
            dma((2, n_y, PARTS)),
            dma((2, n_y - 1, PARTS)),
            dma((2, PARTS)),
            dma((2, n_y - 1, PARTS)),
            dma((2, n_y - 1, PARTS)),
            dma((2, n_z, slabs)),
            dma((2, 2, n_z, slabs)),
            dma((2, 2)),
            dma((2, n_y - 1)),
            dma((2, steps)),
            dma((2, n_col - 1)),
        ],
        compiler_params=pltpu.CompilerParams(
            collective_id=0, has_side_effects=True, vmem_limit_bytes=40 * 1024 * 1024
        ),
    )(block, partial, weight, out_grad)


def on_device(n_row, n_col, tiles, tile_slot, tile_count, feats, weight, out_grad):
    held = [
        pltpu.with_memory_space_constraint(array, pltpu.HBM)
        for array in (tiles[0], tile_slot, feats)
    ]
    block, partial = block_product(held[0], held[1], tile_count, held[2])
    activated, weight_grad, window_grad = exchange(
        n_row, n_col, block, partial, weight, out_grad
    )
    activated, weight_grad, window_grad = publish(activated, weight_grad, window_grad)
    return activated, weight_grad, window_grad[None]


def solution(mesh):
    placed = (
        P("row", "col", None, None),
        P("row", "col"),
        P("row", "col"),
        P("col", None),
        P(),
        P(("row", "col"), None),
    )
    return jax.shard_map(
        functools.partial(on_device, mesh.shape["row"], mesh.shape["col"]),
        mesh=mesh,
        in_specs=placed,
        out_specs=(P(("row", "col"), None), P(), P("col", "row", None)),
        check_vma=False,
    )
```

```python
import functools
import math

import jax
import jax.numpy as jnp
from jax import lax
from jax.experimental import pallas as pl
from jax.experimental.pallas import tpu as pltpu
from jax.sharding import PartitionSpec as P

RT = 4
LANES = 128
PARTS = 2
MESH = pl.DeviceIdType.MESH
F32 = jnp.float32
BF16 = jnp.bfloat16


def block_kernel(slot_list, count, tiles, feats, block, partial, extra, source, total,
                 slots, first, others, following, list_sem, tile_sem, feat_sem):
    size = tiles.shape[1]
    col_tiles = feats.shape[0] // size
    places = RT * col_tiles

    list_copy = pltpu.make_async_copy(slot_list, slots, list_sem)
    list_copy.start()
    feat_copy = pltpu.make_async_copy(feats, source, feat_sem)
    feat_copy.start()

    def place_of(slot):
        row = pl.multiple_of(slot // col_tiles * size, size)
        column = pl.multiple_of(slot % col_tiles * size, size)
        return block.at[pl.ds(row, size), pl.ds(column, size)]

    for place in range(places):
        first[place] = -1
        others[place] = -1
    list_copy.wait()
    live = count[0, 0]

    @pl.loop(0, live)
    def _(position):
        slot = slots[0, position]
        taken = first[slot] >= 0

        @pl.when(jnp.logical_not(taken))
        def _():
            first[slot] = position
            pltpu.make_async_copy(tiles.at[position], place_of(slot), tile_sem.at[position]).start()

        @pl.when(taken)
        def _():
            following[position] = others[slot]
            others[slot] = position
            pltpu.make_async_copy(
                tiles.at[position], extra.at[position], tile_sem.at[position]
            ).start()

    @pl.loop(0, places)
    def _(place):
        @pl.when(first[place] < 0)
        def _():
            place_of(place)[...] = jnp.zeros((size, size), BF16)

    def await_tile(position):
        pltpu.make_async_copy(
            tiles.at[position], extra.at[position], tile_sem.at[position]
        ).wait()

    for row in range(RT):
        @pl.loop(row * col_tiles, (row + 1) * col_tiles)
        def _(place):
            @pl.when(first[place] >= 0)
            def _():
                await_tile(first[place])

                @pl.when(others[place] >= 0)
                def _():
                    spot = place_of(place)
                    total[...] = spot[...].astype(F32)

                    def add(position):
                        await_tile(position)
                        total[...] += extra[position].astype(F32)
                        return following[position]

                    lax.while_loop(lambda position: position >= 0, add, others[place])
                    spot[...] = total[...].astype(BF16)

        if row % 2 == 1:
            if row == 1:
                feat_copy.wait()
            rows = pl.ds((row - 1) * size, 2 * size)
            partial[rows, :] = jnp.dot(
                block[rows, :], source[...], preferred_element_type=F32
            ).astype(BF16)


def block_product(tiles, slots, count, feats):
    number, size, _ = tiles.shape
    window, width = feats.shape
    places = RT * window // size
    hbm = pl.BlockSpec(memory_space=pltpu.HBM)
    vmem = pl.BlockSpec(memory_space=pltpu.VMEM)
    return pl.pallas_call(
        block_kernel,
        out_shape=(
            jax.ShapeDtypeStruct((RT * size, window), BF16),
            jax.ShapeDtypeStruct((RT * size, width), BF16),
        ),
        in_specs=[hbm, pl.BlockSpec(memory_space=pltpu.SMEM), hbm, hbm],
        out_specs=(vmem, vmem),
        scratch_shapes=[
            pltpu.VMEM((number, size, size), BF16),
            pltpu.VMEM((window, width), BF16),
            pltpu.VMEM((size, size), F32),
            pltpu.SMEM(slots.shape, jnp.int32),
            pltpu.SMEM((places,), jnp.int32),
            pltpu.SMEM((places,), jnp.int32),
            pltpu.SMEM((number,), jnp.int32),
            pltpu.SemaphoreType.DMA,
            pltpu.SemaphoreType.DMA((number,)),
            pltpu.SemaphoreType.DMA,
        ],
        compiler_params=pltpu.CompilerParams(vmem_limit_bytes=24 * 1024 * 1024),
    )(slots, count, tiles, feats)


def publish_kernel(*refs):
    number = len(refs) // 2
    sem = refs[-1]
    copies = [
        pltpu.make_async_copy(refs[i], refs[number + i], sem.at[i]) for i in range(number)
    ]
    for copy in copies:
        copy.start()
    for copy in copies:
        copy.wait()


def publish(*results):
    held = [pltpu.with_memory_space_constraint(r, pltpu.VMEM) for r in results]
    return pl.pallas_call(
        publish_kernel,
        out_shape=tuple(jax.ShapeDtypeStruct(r.shape, r.dtype) for r in results),
        in_specs=[pl.BlockSpec(memory_space=pltpu.VMEM)] * len(results),
        out_specs=tuple(pl.BlockSpec(memory_space=pltpu.HBM) for _ in results),
        scratch_shapes=[pltpu.SemaphoreType.DMA((len(results),))],
    )(*held)


def remote(src, dst, send_sem, recv_sem, device):
    return pltpu.make_async_remote_copy(
        src_ref=src, dst_ref=dst, send_sem=send_sem, recv_sem=recv_sem,
        device_id=device, device_id_type=MESH,
    )


def slabs_of(rows):
    return 4 if rows % 64 == 0 else 2


def exchange_kernel(n_row, n_col, scale, block, partial, weight, out_grad,
                    activated, weight_grad, window_grad,
                    core_in, pair_out, pair_in, grads, grads_wide, cross_out, cross_in,
                    chain_out, chain_in, total, ready, local, local_out, piece_in, piece, step_in, whole,
                    core_sem, pair_sem, own_sem, far_sem, pass_sem, cross_sem,
                    chain_sem, piece_sem, step_sem, whole_sem):
    n_z, n_y = n_row // 2, n_col // 2
    row, col = lax.axis_index("row"), lax.axis_index("col")
    z, x = row // 2, row % 2
    y, core = col // 2, col % 2
    share = out_grad.shape[0]
    span = window_grad.shape[0]
    width = weight.shape[0]
    depth = width // n_col
    steps = n_row.bit_length() - 1
    cut = share // PARTS

    sibling = (row, y * 2 + 1 - core)
    mirror = (z * 2 + 1 - x, col)
    col_peers = [(row, (col + d) % n_col) for d in range(1, n_col)]
    swaps = []
    for s in range(steps):
        bit = 1 << s
        swaps.append((row + bit - row // bit % 2 * 2 * bit, col))
    ring = [((row + 2) % n_row, col), ((row + n_row - 2) % n_row, col)]

    barrier = pltpu.get_barrier_semaphore()
    greeted = col_peers + swaps + ring
    for device in greeted:
        pl.semaphore_signal(barrier, inc=1, device_id=device, device_id_type=MESH)
    pl.semaphore_wait(barrier, len(greeted))

    started = []

    def send(*args):
        copy = remote(*args)
        copy.start()
        started.append(copy)
        return copy

    def rows_of(index, length):
        if isinstance(index, int):
            return pl.ds(index * length, length)
        return pl.ds(pl.multiple_of(index * length, length), length)

    def part_of(owner, part):
        return rows_of(owner * PARTS + part, cut)

    core_copies = {}
    for d in list(range(1, n_y)) + [0]:
        for part in range(PARTS):
            owner = (y + d) % n_y * 2 + 1 - core
            core_copies[d, part] = send(
                partial.at[part_of(owner, part)], core_in.at[d, part],
                core_sem.at[0, d, part], core_sem.at[1, d, part], sibling)
    pair_copies = {}
    for part in range(PARTS):
        for d in range(1, n_y):
            core_copies[d, part].wait_recv()
            owner = (y + d) % n_y * 2 + core
            pair_out[d - 1, part] = (
                partial[part_of(owner, part), :].astype(F32) + core_in[d, part].astype(F32)
            ).astype(BF16)
            pair_copies[d, part] = send(
                pair_out.at[d - 1, part], pair_in.at[d - 1, part],
                pair_sem.at[0, d - 1, part], pair_sem.at[1, d - 1, part], (row, owner))

    far_copies, own_copies = {}, []
    for part in range(PARTS):
        core_copies[0, part].wait_recv()
        sums = partial[part_of(col, part), :].astype(F32) + core_in[0, part].astype(F32)
        for d in range(1, n_y):
            pair_copies[d, part].wait_recv()
            sums = sums + pair_in[d - 1, part].astype(F32)
        aggregated = sums.astype(BF16)
        pre_act = jnp.dot(aggregated, weight[...], preferred_element_type=F32)
        sigmoid_pre = jax.nn.sigmoid(pre_act)
        rows = pl.ds(part * cut, cut)
        grad_pre = (
            out_grad[rows, :].astype(F32) * sigmoid_pre * (1.0 + pre_act * (1.0 - sigmoid_pre))
        ).astype(BF16)
        grads[col, part] = lax.dot_general(
            weight[...], grad_pre, (((1,), (1,)), ((), ())), preferred_element_type=F32
        ).astype(BF16)
        mine = grads.at[col, part]
        for d in range(1, n_y):
            far_copies[d, part] = send(
                mine, mine, far_sem.at[0, d - 1, part], far_sem.at[1, d - 1, part],
                (row, (y + d) % n_y * 2 + core))
        own_copies.append(send(mine, mine, own_sem.at[0, part], own_sem.at[1, part], sibling))
        activated[rows, :] = (pre_act * sigmoid_pre).astype(BF16)
        outer = lax.dot_general(
            aggregated, grad_pre, (((0,), (0,)), ((), ())), preferred_element_type=F32
        )
        if part == 0:
            local[...] = outer
        else:
            local[...] += outer

    pass_copies = []
    for part in range(PARTS):
        for d in range(1, n_y):
            far_copies[d, part].wait_recv()
            got = grads.at[(y + n_y - d) % n_y * 2 + core, part]
            pass_copies.append(send(
                got, got, pass_sem.at[0, d - 1, part], pass_sem.at[1, d - 1, part], sibling))
    local_out[...] = local[...].astype(BF16)
    piece_copies = []
    for d in range(1, n_col):
        piece_copies.append(send(
            local_out.at[rows_of((col + d) % n_col, depth)], piece_in.at[d - 1],
            piece_sem.at[0, d - 1], piece_sem.at[1, d - 1], col_peers[d - 1]))
    for copy in own_copies + pass_copies:
        copy.wait_recv()
    for owner in range(n_col):
        for part in range(PARTS):
            grads_wide[:, part_of(owner, part)] = grads[owner, part]

    def columns_product(index, length):
        return jnp.dot(
            grads_wide[...], block[:, rows_of(index, length)], preferred_element_type=F32
        )

    narrow = span % LANES != 0
    if narrow:
        for tile in range(block.shape[1] // width):
            ready[rows_of(tile, width), :] = columns_product(tile, width).T

    def product(owner):
        if narrow:
            return ready[rows_of(owner, span), :]
        return columns_product(owner, span)

    high = (2 * z >= n_z).astype(jnp.int32)
    low_z = z + high * (n_z - 1 - 2 * z)

    def order(i):
        lead = n_z - 1 - 2 * low_z
        m = i - lead
        early = (m < 0).astype(jnp.int32)
        odd = jnp.abs(m) % 2
        late = (1 - odd) * (m // 2) + odd * (2 * low_z - m // 2)
        at = early * (n_z - 1 - i) + (1 - early) * late
        return at + high * (n_z - 1 - 2 * at)

    slabs = slabs_of(total.shape[0])
    slab = total.shape[0] // slabs

    def cross_copy(at, part):
        rows = pl.ds(part * slab, slab)
        return (cross_out.at[at, rows], cross_in.at[at, rows],
                cross_sem.at[0, at, part], cross_sem.at[1, at, part], mirror)

    swap_copies, whole_copies = [], []

    def next_swap(s):
        if s == 0:
            added = local[rows_of(col, depth), :]
            for copy in piece_copies:
                copy.wait_recv()
            for d in range(1, n_col):
                added = added + piece_in[d - 1].astype(F32)
        elif s <= steps:
            swap_copies[s - 1].wait_recv()
            added = piece[s - 1].astype(F32) + step_in[s - 1].astype(F32)
        if s < steps:
            piece[s] = added.astype(BF16)
            swap_copies.append(send(
                piece.at[s], step_in.at[s], step_sem.at[0, s], step_sem.at[1, s], swaps[s]))
        elif s == steps:
            spot = whole.at[rows_of(col, depth)]
            spot[...] = (added * scale).astype(BF16)
            for d in range(1, n_col):
                whole_copies.append(send(
                    spot, spot, whole_sem.at[0, d - 1], whole_sem.at[1, d - 1],
                    col_peers[d - 1]))

    def chain_copy(at, part):
        rows = pl.ds(part * slab, slab)
        up = (at > z).astype(jnp.int32)
        return remote(chain_out.at[at, rows], chain_in.at[up, at, rows],
                      chain_sem.at[0, up, at, part], chain_sem.at[1, up, at, part],
                      (row + 4 * up - 2, col))

    def await_chain(up, at, part):
        rows = pl.ds(part * slab, slab)
        remote(chain_out.at[at, rows], chain_in.at[up, at, rows],
               chain_sem.at[0, up, at, part], chain_sem.at[1, up, at, part], mirror).wait_recv()
        total[rows, :] += chain_in[up, at, rows, :].astype(F32)

    for i in range(n_z):
        at = order(i)
        cross_out[at] = product(at * 2 + 1 - x).astype(BF16)
        for part in range(slabs):
            send(*cross_copy(at, part))
        if i == min(1, n_z - 1):
            next_swap(0)
    for i in range(n_z):
        at = order(i)
        total[...] = product(at * 2 + x)
        for part in range(slabs):
            rows = pl.ds(part * slab, slab)
            remote(*cross_copy(at, part)).wait_recv()
            total[rows, :] += cross_in[at, rows, :].astype(F32)

            @pl.when(jnp.logical_and(z > 0, at >= z))
            def _():
                await_chain(1, at, part)

            @pl.when(jnp.logical_and(z < n_z - 1, at <= z))
            def _():
                await_chain(0, at, part)

            if i < n_z - 1:
                chain_out[at, rows, :] = total[rows, :].astype(BF16)
                chain_copy(at, part).start()
        if i == n_z - 1:
            result = total[...] if narrow else total[...].T
            window_grad[...] = result.astype(BF16)
        next_swap(i + 1)
    for s in range(n_z + 1, steps + 1):
        next_swap(s)
    for copy in whole_copies:
        copy.wait_recv()
    weight_grad[...] = whole[...].astype(F32)
    for copy in started:
        copy.wait_send()
    for i in range(n_z - 1):
        for part in range(slabs):
            chain_copy(order(i), part).wait_send()


def exchange(n_row, n_col, block, partial, weight, out_grad):
    rows, window = block.shape
    width = weight.shape[0]
    share = out_grad.shape[0]
    span = window // n_row
    n_z, n_y = n_row // 2, n_col // 2
    depth = width // n_col
    steps = n_row.bit_length() - 1
    cut = share // PARTS
    narrow = span % LANES != 0
    chunk = (span, width) if narrow else (width, span)
    slabs = slabs_of(chunk[0])
    dma = pltpu.SemaphoreType.DMA
    vmem = pl.BlockSpec(memory_space=pltpu.VMEM)
    return pl.pallas_call(
        functools.partial(exchange_kernel, n_row, n_col, 1.0 / math.sqrt(rows * n_row)),
        out_shape=(
            jax.ShapeDtypeStruct((share, width), BF16),
            jax.ShapeDtypeStruct((width, width), F32),
            jax.ShapeDtypeStruct((span, width), BF16),
        ),
        in_specs=[vmem, vmem, vmem, vmem],
        out_specs=(vmem, vmem, vmem),
        scratch_shapes=[
            pltpu.VMEM((n_y, PARTS, cut, width), BF16),
            pltpu.VMEM((n_y - 1, PARTS, cut, width), BF16),
            pltpu.VMEM((n_y - 1, PARTS, cut, width), BF16),
            pltpu.VMEM((n_col, PARTS, width, cut), BF16),
            pltpu.VMEM((width, rows), BF16),
            pltpu.VMEM((n_z, *chunk), BF16),
            pltpu.VMEM((n_z, *chunk), BF16),
            pltpu.VMEM((n_z, *chunk), BF16),
            pltpu.VMEM((2, n_z, *chunk), BF16),
            pltpu.VMEM(chunk, F32),
            pltpu.VMEM((window if narrow else 8, width), F32),
            pltpu.VMEM((width, width), F32),
            pltpu.VMEM((width, width), BF16),
            pltpu.VMEM((n_col - 1, depth, width), BF16),
            pltpu.VMEM((steps, depth, width), BF16),
            pltpu.VMEM((steps, depth, width), BF16),
            pltpu.VMEM((width, width), BF16),
            dma((2, n_y, PARTS)),
            dma((2, n_y - 1, PARTS)),
            dma((2, PARTS)),
            dma((2, n_y - 1, PARTS)),
            dma((2, n_y - 1, PARTS)),
            dma((2, n_z, slabs)),
            dma((2, 2, n_z, slabs)),
            dma((2, n_col - 1)),
            dma((2, steps)),
            dma((2, n_col - 1)),
        ],
        compiler_params=pltpu.CompilerParams(
            collective_id=0, has_side_effects=True, vmem_limit_bytes=40 * 1024 * 1024
        ),
    )(block, partial, weight, out_grad)


def on_device(n_row, n_col, tiles, tile_slot, tile_count, feats, weight, out_grad):
    held = [
        pltpu.with_memory_space_constraint(array, pltpu.HBM)
        for array in (tiles[0], tile_slot, feats)
    ]
    block, partial = block_product(held[0], held[1], tile_count, held[2])
    activated, weight_grad, window_grad = exchange(
        n_row, n_col, block, partial, weight, out_grad
    )
    activated, weight_grad, window_grad = publish(activated, weight_grad, window_grad)
    return activated, weight_grad, window_grad[None]


def solution(mesh):
    placed = (
        P("row", "col", None, None),
        P("row", "col"),
        P("row", "col"),
        P("col", None),
        P(),
        P(("row", "col"), None),
    )
    return jax.shard_map(
        functools.partial(on_device, mesh.shape["row"], mesh.shape["col"]),
        mesh=mesh,
        in_specs=placed,
        out_specs=(P(("row", "col"), None), P(), P("col", "row", None)),
        check_vma=False,
    )
```
